128 devices in a mesh: gx: 4 (over y), gy: 4 (over x_hi, core), gz: 8 (over z, x_lo).
Axes of the slice: x: 4 (x_hi: 2, x_lo: 2; x = x_hi * 2 + x_lo), y: 4, z: 4, core: 2. Of those that a mesh axis runs over, the one named last changes fastest.
Arguments:
- initial_state: float32 [2, 4, 4, 8, 131072], P(None, 'gx', 'gy', 'gz'), may hold values from -6 to 6
- local_gates: float32 [3, 2, 128, 128], replicated, may hold values from -0.375 to 0.375
- top_gates: float32 [2, 2, 128, 128], replicated, may hold values from -1 to 1
- placement: int32 [5, 7], replicated, may hold values from 0 to 6, each once within a row
- damping: float32 [7], replicated, may hold values from 0.05 to 0.5
- branches: int32 [7], replicated, may hold values from 0 to 1
- outcomes: int32 [4], replicated, may hold values from 0 to 1, as said below
Outputs:
- collapsed: float32 [2, 4, 4, 8, 131072], P(None, 'gx', 'gy', 'gz')
- probability: float32 [], replicated
The draws below stay inside these ranges and needn't reach their ends.
Inputs may be any that keep to these rules, and one draw needn't show every extreme that they name: `placement`: each row is a permutation of 0 to 6. `outcomes`: the four entries are not all equal.
All inputs are finite; a program needn't handle non-finite values.
Results may differ from the reference program's by a relative error of at most 0.0003.
Values sent between devices are 32-bit elements; how exact they have to be, the bound alone decides.
A program may use at most 64 MiB of HBM per device.

```python
import math
import jax
import jax.numpy as jnp
from jax import lax

AMP_DEV = 131072
GATE_DIM = 128
NOISE_SITES = 7
AMPS = 16777216
N_GX = 4
N_GY = 4
N_GZ = 8


def draw_top_gates(key, part):
    key = jax.random.fold_in(key, 7)
    key_entries, key_rows = jax.random.split(key)
    entries = jnp.clip(jax.random.normal(key_entries, (2, 2, 128, 128), jnp.float32), -5.0, 5.0)
    row_scale = jnp.exp(jax.random.uniform(key_rows, (2, 1, 128, 1), jnp.float32, 0.0, 1.1))
    return entries * row_scale / 16.0


def draw_outcomes(key, part):
    key = jax.random.fold_in(key, 11)
    pattern = jax.random.randint(key, (), 1, 15, jnp.int32)
    places = jnp.arange(4, dtype=jnp.int32)
    return jnp.bitwise_and(jnp.right_shift(pattern, 3 - places), 1)


def set_ends(values, stream_key, low, high):
    dims = values.shape
    spot = [jax.random.randint(jax.random.fold_in(stream_key, axis), (), 0, dims[axis]) for axis in range(len(dims))]
    values = values.at[tuple(spot)].set(low)
    longest = dims.index(max(dims))
    spot[longest] = (spot[longest] + 1) % dims[longest]
    return values.at[tuple(spot)].set(high)


def level_of(stream_key, shape, pieces, smallest, high):
    factor_of, own = 1.0, jax.random.fold_in(stream_key, 6)
    for position, blocks in pieces:
        draws = jnp.exp(jax.random.uniform(jax.random.fold_in(own, position), (blocks,), jnp.float32, smallest / len(pieces), high / len(pieces)))
        factor_of = factor_of * jnp.repeat(draws, shape[position] // blocks).reshape([-1 if axis == position else 1 for axis in range(len(shape))])
    return factor_of


def centred(rng, dims, width, most, cuts=(), kind=jnp.bfloat16):
    factor_of = level_of(rng, dims, cuts, -0.22, 0.18) if cuts else 1.0
    values = jax.random.normal(rng, dims, jnp.float32) * width * factor_of
    return jnp.minimum(jnp.maximum(values, -most), most).astype(kind)


def setup_inputs(seed: int = 0) -> dict:
    key_of = jax.random.split(jax.random.key(seed), 8)
    return {
        "initial_state": centred(key_of[0], (2, N_GX, N_GY, N_GZ, AMP_DEV), 1.0, 6.0, ((1, 4), (2, 4), (3, 8)), jnp.float32),
        "local_gates": centred(key_of[1], (3, 2, GATE_DIM, GATE_DIM), (2 * GATE_DIM) ** -0.5, 0.375, (), jnp.float32),
        "top_gates": draw_top_gates(jax.random.fold_in(key_of[7], 71), 0),
        "placement": jax.vmap(lambda own: jax.random.permutation(own, NOISE_SITES))(jax.random.split(key_of[3], 5)).reshape((5, NOISE_SITES)).astype(jnp.int32),
        "damping": jnp.clip(jnp.exp(jax.random.uniform(key_of[4], (NOISE_SITES,), jnp.float32, math.log(0.05), math.log(0.5))), 0.05, 0.5),
        "branches": set_ends(jax.random.randint(key_of[5], (NOISE_SITES,), 0, 2), jax.random.fold_in(key_of[5], 1), 0, 1).astype(jnp.int32),
        "outcomes": draw_outcomes(jax.random.fold_in(key_of[7], 71), 0),
    }


def oriented(gate, leg_order):
    lanes = jnp.arange(128, dtype=jnp.int32)
    source = jnp.zeros((128,), jnp.int32)
    for bit_pos in range(7):
        picked = jnp.bitwise_and(jnp.right_shift(lanes, leg_order[bit_pos]), 1)
        source = source + jnp.left_shift(picked, bit_pos)
    selector_matrix = (source[:, None] == lanes[None, :]).astype(jnp.float32)
    highest = lax.Precision.HIGHEST
    return tuple((jnp.dot(jnp.dot(selector_matrix, gate[part_index], precision=highest), selector_matrix.T, precision=highest) for part_index in range(2)))

def kraus_matrix(damping, branches):
    lanes = jnp.arange(128, dtype=jnp.int32)
    result = jnp.ones((128, 128), jnp.float32)
    for bit_pos in range(7):
        row_bit = jnp.bitwise_and(jnp.right_shift(lanes, bit_pos), 1)[:, None]
        col_bit = jnp.bitwise_and(jnp.right_shift(lanes, bit_pos), 1)[None, :]
        staying = jnp.where(row_bit == col_bit, jnp.where(row_bit == 1, jnp.sqrt(1.0 - damping[bit_pos]), 1.0), 0.0)
        jumping = jnp.where((row_bit == 0) & (col_bit == 1), jnp.sqrt(damping[bit_pos]), 0.0)
        result = result * jnp.where(branches[bit_pos] == 0, staying, jumping)
    return result

def product(matrix, vector):
    return jnp.einsum('kj,ajr->akr', matrix, vector, precision=lax.Precision.HIGHEST)

def apply_block(real_part, imag_part, matrix, low):
    real_view = real_part.reshape(-1, 128, 2 ** low)
    imag_view = imag_part.reshape(-1, 128, 2 ** low)
    new_real = product(matrix[0], real_view) - product(matrix[1], imag_view)
    new_imag = product(matrix[0], imag_view) + product(matrix[1], real_view)
    return (new_real.reshape(-1), new_imag.reshape(-1))

def reference(initial_state, local_gates, top_gates, placement, damping, branches, outcomes):
    local_bits = AMP_DEV.bit_length() - 1
    global_bits = (N_GX * N_GY * N_GZ).bit_length() - 1
    qubits = local_bits + global_bits
    real_part = initial_state[0].reshape(-1)
    imag_part = initial_state[1].reshape(-1)
    matrices = [oriented(local_gates[0], placement[0]), oriented(local_gates[1], placement[1]), oriented(top_gates[0], placement[2]), oriented(local_gates[2], placement[3]), oriented(top_gates[1], placement[4])]
    lows = [0, local_bits - 7, qubits - 7, 0, qubits - 7]
    for matrix, low in zip(matrices, lows):
        real_part, imag_part = apply_block(real_part, imag_part, matrix, low)
    kraus = kraus_matrix(damping, branches)
    real_part = product(kraus, real_part.reshape(-1, 128, 1)).reshape(-1)
    imag_part = product(kraus, imag_part.reshape(-1, 128, 1)).reshape(-1)
    norm_five = jnp.sum(real_part * real_part) + jnp.sum(imag_part * imag_part)
    scaling = jnp.sqrt(AMPS / norm_five)
    real_part = real_part * scaling
    imag_part = imag_part * scaling
    sixteen = jnp.arange(16, dtype=jnp.int32)
    matched = jnp.ones((16,), jnp.bool_)
    for which in range(4):
        matched = matched & (jnp.bitwise_and(jnp.right_shift(sixteen, 3 - which), 1) == outcomes[which])
    selector = matched.astype(jnp.float32)
    proj_real = real_part.reshape(16, -1) * selector[:, None]
    proj_imag = imag_part.reshape(16, -1) * selector[:, None]
    probability = (jnp.sum(proj_real * proj_real) + jnp.sum(proj_imag * proj_imag)) / AMPS
    root = jnp.sqrt(probability)
    collapsed = jnp.stack([proj_real / root, proj_imag / root]).reshape(initial_state.shape)
    return (collapsed, probability)
```

```python
import functools

import jax
import jax.numpy as jnp
from jax import lax
from jax.experimental import pallas as pl
from jax.experimental.pallas import tpu as pltpu
from jax.sharding import PartitionSpec as P

F32 = jnp.float32
BF16 = jnp.bfloat16
I32 = jnp.int32
MESH = pl.DeviceIdType.MESH
TOTAL = 16777216.0


def split(a):
    high = a.astype(BF16)
    return high, (a - high.astype(F32)).astype(BF16)


def mm(a, b, transposed=False):
    dims = (((1,), (1 if transposed else 0,)), ((), ()))
    return lax.dot_general(a, b, dims, preferred_element_type=F32)


def dot_split(a, b, transposed=False):
    return mm(a[0], b[0], transposed) + (mm(a[0], b[1], transposed) + mm(a[1], b[0], transposed))


def dot3(a, b, transposed=False):
    return dot_split(split(a), split(b), transposed)


def permuted_rows(onehot, b):
    high, low = split(b)
    return mm(onehot, high) + mm(onehot, low)


def permuted_columns(a, onehot):
    high, low = split(a)
    return mm(high, onehot) + mm(low, onehot)


def lanes(width=128):
    return lax.broadcasted_iota(I32, (1, width), 1)


def source(legs, k):
    out = jnp.zeros_like(k)
    for i in range(7):
        out = out | (((k >> legs[i]) & 1) << i)
    return out


def unsource(legs, s):
    out = jnp.zeros_like(s)
    for i in range(7):
        out = out | (((s >> i) & 1) << legs[i])
    return out


def hits(target, rows=128):
    return lax.broadcasted_iota(I32, (rows, target.shape[1]), 0) == target


def onehot(target, rows=128):
    return jnp.where(hits(target, rows), 1.0, 0.0).astype(BF16)


def compact_index(branches, j):
    out = jnp.zeros_like(j)
    count = jnp.int32(0)
    for i in range(7):
        stays = 1 - branches[i]
        out = out | ((((j >> i) & 1) * stays) << count)
        count = count + stays
    return out


def kraus_weight(branches, damping, j):
    weight = jnp.ones(j.shape, F32)
    for i in range(7):
        bit = ((j >> i) & 1) == 1
        d = jnp.full(j.shape, damping[i], F32)
        root = jnp.sqrt(jnp.where(branches[i] == 0, 1.0 - d, d))
        off = jnp.where(branches[i] == 0, 1.0, 0.0)
        weight = weight * jnp.where(bit, root, off)
    return weight


def complex_rows(pair):
    half = pair.shape[0] // 2
    r, i = pair[:half], pair[half:]
    return jnp.concatenate(
        [jnp.concatenate([r, -i], axis=1), jnp.concatenate([i, r], axis=1)], axis=0
    )


def complex_columns(pair):
    half = pair.shape[1] // 2
    r, i = pair[:, :half], pair[:, half:]
    return jnp.concatenate(
        [jnp.concatenate([r, i], axis=1), jnp.concatenate([-i, r], axis=1)], axis=0
    )


def side(gate_ref, which):
    return jnp.concatenate([gate_ref[which, 0], gate_ref[which, 1]], axis=1)


def stack_halves(pair):
    half = pair.shape[1] // 2
    return jnp.concatenate([pair[:, :half], pair[:, half:]], axis=0)


def side_halves(pair):
    half = pair.shape[0] // 2
    return jnp.concatenate([pair[:half], pair[half:]], axis=1)


HOPS = (0, 1, 2, 1)


def hops(offset):
    dy, dh, dz, dl = offset
    return HOPS[dy] + HOPS[dz] + (2 if (dh, dl) == (1, 0) else dh | dl)


CHIPS = [
    (dy, dh, dz, dl)
    for dy in range(4)
    for dh in range(2)
    for dz in range(4)
    for dl in range(2)
    if dy or dh or dz or dl
]
FAR = [sorted((o for o in CHIPS if hops(o) in at), key=hops, reverse=True) for at in ((6, 5), (4,))]
NEAR = [[o for o in CHIPS if hops(o) == at] for at in (3, 2, 1)]


def each_core(classes, act):
    for offsets in classes:

        @pl.loop(0, 2)
        def _(other, offsets=offsets):
            for offset in offsets:
                act(offset, other)


OWNERS = [
    (f, dh, dz, dl)
    for f in (1, 0)
    for dh in range(2)
    for dz in range(4)
    for dl in range(2)
    if f or dh or dz or dl
]
OWNER_CLASSES = [[o for o in OWNERS if hops(o) in at] for at in ((5,), (4,), (3,), (2,), (1,))]


def each_owner(place, act):
    each_core(OWNER_CLASSES, act)
    act((0, 0, 0, 0), 1)

    @pl.when(jnp.logical_not(place.owner))
    def _():
        act((0, 0, 0, 0), 0)


def each_other(act):
    each_core(FAR + NEAR, act)
    act((0, 0, 0, 0), 1)


class Place:
    def __init__(self):
        gx, gy, gz = (lax.axis_index(name) for name in ("gx", "gy", "gz"))
        self.index = (gx * 4 + gy) * 8 + gz
        self.row, self.column = gx * 4 + gy, gz
        self.core, xh = lax.rem(gy, 2), lax.div(gy, 2)
        z, xl = lax.div(gz, 2), lax.rem(gz, 2)
        self.ys = [gx] + [lax.rem(gx + d, 4) for d in (1, 2, 3)]
        zs = [z] + [lax.rem(z + d, 4) for d in (1, 2, 3)]
        self.owner = gx < 2
        near = lax.div(lax.rem(gx + 1, 4), 2)
        self.owner_ys = [near, 1 - near]
        self.xhs = [xh * 2, 2 - xh * 2]
        xls = [xl, 1 - xl]
        self.gzs = [[zs[dz] * 2 + xls[dl] for dl in range(2)] for dz in range(4)]

    def device(self, offset, other):
        dy, dh, dz, dl = offset
        core = self.core + other * (1 - 2 * self.core)
        return (self.ys[dy], self.xhs[dh] + core, self.gzs[dz][dl])

    def owner_device(self, offset, other):
        f, dh, dz, dl = offset
        core = self.core + other * (1 - 2 * self.core)
        return (self.owner_ys[f], self.xhs[dh] + core, self.gzs[dz][dl])

    def column_of(self, offset):
        return self.gzs[offset[2]][offset[3]]

    def index_of(self, offset, other):
        gx, gy, gz = self.device(offset, other)
        return (gx * 4 + gy) * 8 + gz


def block(ref, index, rows):
    return ref.at[pl.ds(index * rows, rows)]


def wait_for(ref, rows, sem):
    part = ref.at[pl.ds(0, rows)]
    pltpu.make_async_copy(part, part, sem).wait()


def layout(level):
    shared = level > 3
    return shared, 1 if shared else 2, max(8 >> level, 1), 128 >> level


def main_kernel(
    level,
    x_hbm,
    local_hbm,
    top_hbm,
    placement_hbm,
    damping_hbm,
    branches_hbm,
    outcomes_hbm,
    f_ref,
    packed_ref,
    chosen_ref,
    p_ref,
    x_ref,
    local_ref,
    top_ref,
    placement,
    damping,
    branches,
    outcomes,
    out_buf,
    in_buf,
    back_out,
    back_in,
    in_sem,
    send_sem,
    recv_sem,
    own_sem,
    ready_sem,
):
    shared, parts, groups, width = layout(level)
    per_block = 2 if shared else parts * groups
    per_back = per_block + 1
    place = Place()

    barrier = pltpu.get_barrier_semaphore()

    def enter(offset, other):
        pl.semaphore_signal(
            barrier, inc=1, device_id=place.device(offset, other), device_id_type=MESH
        )

    if shared:
        pl.when(place.owner)(lambda: each_other(enter))
    else:
        each_core(FAR, enter)
    loads = [
        pltpu.make_async_copy(src, dst, in_sem.at[n])
        for n, (src, dst) in enumerate(
            (
                (branches_hbm, branches),
                (damping_hbm, damping),
                (placement_hbm, placement),
                (outcomes_hbm, outcomes),
                (local_hbm, local_ref),
                (x_hbm, x_ref),
                (top_hbm, top_ref),
            )
        )
    ]
    for load in loads:
        load.start()
    if not shared:
        each_core(NEAR, enter)
        enter((0, 0, 0, 0), 1)
    for load in loads[:6]:
        load.wait()

    legs = [[placement[t, i] for i in range(7)] for t in range(5)]
    branch = [branches[i] for i in range(7)]
    damp = [damping[i] for i in range(7)]
    lane = lanes()

    after = unsource(legs[3], lane)
    left = jnp.where(
        hits(compact_index(branch, after), width), kraus_weight(branch, damp, after), 0.0
    )
    left = dot3(left, side(local_ref, 2))
    right = permuted_rows(
        onehot(source(legs[3], unsource(legs[0], lane))), side(local_ref, 0)
    )
    right = permuted_columns(stack_halves(right), onehot(source(legs[0], lane)))
    low = stack_halves(dot3(left, complex_columns(side_halves(right))))
    low = split(complex_rows(low))

    mid = permuted_rows(onehot(unsource(legs[1], lane)), side(local_ref, 1))
    mid = permuted_columns(stack_halves(mid), onehot(source(legs[1], lane)))
    mid = complex_rows(mid)
    mid = split(mid[:128] if shared else mid)

    rows = jnp.concatenate(
        [
            jnp.concatenate(
                [x_ref[pl.ds(q, 128, stride=8), :], x_ref[pl.ds(1024 + q, 128, stride=8), :]], axis=1
            )
            for q in range(8)
        ],
        axis=0,
    )
    z = dot_split(low, split(rows), transposed=True)
    for g in range(groups):
        pieces, turned = [], []
        for u in range(8 // groups):
            q = g * (8 // groups) + u
            piece = z[:, q * 128 : q * 128 + 128]
            r, i = piece[:width], piece[width:]
            pieces.append(jnp.concatenate([r, i], axis=1))
            turned.append(jnp.concatenate([i, -r], axis=1))
        if shared:
            pieces = pieces + turned
        y = dot_split(mid, split(jnp.concatenate(pieces, axis=0)), transposed=True)
        if shared:
            for block_of in range(2):
                out_buf[pl.ds(block_of, 64, stride=2), :] = y[block_of * 64 : block_of * 64 + 64]
            continue
        for part in range(parts):
            out_buf[pl.ds(part * groups + g, 128, stride=per_block), :] = y[
                part * 128 : part * 128 + 128
            ]

    if shared:
        pl.when(place.owner)(lambda: pl.semaphore_wait(barrier, 63))
        pl.when(jnp.logical_not(place.owner))(lambda: pl.semaphore_wait(barrier, 64))
    else:
        pl.semaphore_wait(barrier, 127)

    def send(offset, other):
        pltpu.make_async_remote_copy(
            src_ref=block(out_buf, place.index_of(offset, other), per_block),
            dst_ref=block(in_buf, place.index, per_block),
            send_sem=send_sem.at[0],
            recv_sem=recv_sem.at[0],
            device_id=place.device(offset, other),
            device_id_type=MESH,
        ).start()

    own = pltpu.make_async_copy(
        block(out_buf, place.index, per_block), block(in_buf, place.index, per_block), own_sem.at[0]
    )

    def send_owner(offset, other):
        gx, gy, gz = device = place.owner_device(offset, other)
        pltpu.make_async_remote_copy(
            src_ref=block(out_buf, (gx * 4 + gy) * 8 + gz, 2),
            dst_ref=block(in_buf, place.index, 2),
            send_sem=send_sem.at[0],
            recv_sem=recv_sem.at[0],
            device_id=device,
            device_id_type=MESH,
        ).start()

    def tell_owner(offset, other):
        pl.semaphore_signal(
            ready_sem, inc=1, device_id=place.owner_device(offset, other), device_id_type=MESH
        )

    if shared:
        each_owner(place, send_owner)
        pl.when(jnp.logical_not(place.owner))(lambda: each_owner(place, tell_owner))
    else:
        each_other(send)
        own.start()

    loads[6].wait()
    zero_row = jnp.zeros_like(lane)
    for n in range(7):
        zero_row = zero_row | (((lane >> n) & 1) * branch[n])
    packed_ref[...] = jnp.where(zero_row == 0, compact_index(branch, lane), -1)

    top = permuted_rows(onehot(unsource(legs[4], lane)), side(top_ref, 1))
    top = permuted_columns(
        stack_halves(top), onehot(source(legs[4], unsource(legs[2], lane)))
    )
    top = dot3(side_halves(top), complex_columns(side(top_ref, 0)))
    top = permuted_columns(stack_halves(top), onehot(source(legs[2], lane)))
    top = split(side_halves(top) if shared else complex_rows(top))
    chosen = outcomes[0] * 8 + outcomes[1] * 4 + outcomes[2] * 2 + outcomes[3]

    first_half = lane < 64

    def send_back(offset, other):
        pltpu.make_async_remote_copy(
            src_ref=block(back_out, place.column_of(offset), per_back),
            dst_ref=block(back_in, place.index, per_back),
            send_sem=send_sem.at[1],
            recv_sem=recv_sem.at[1],
            device_id=place.device(offset, other),
            device_id_type=MESH,
        ).start()

    own_back = pltpu.make_async_copy(
        block(back_out, place.column, per_back), block(back_in, place.index, per_back), own_sem.at[1]
    )

    def fold(norm, kept):
        return jnp.where(
            first_half, norm + pltpu.roll(norm, 64, axis=1), kept + pltpu.roll(kept, 64, axis=1)
        )

    def finish(sums, rows):
        sums = jnp.sum(sums, axis=0, keepdims=True)
        norm = jnp.sum(jnp.where(first_half, sums, 0.0), keepdims=True)
        kept = jnp.sum(jnp.where(first_half, 0.0, sums), keepdims=True)
        probability = kept / norm
        scale = jnp.sqrt(TOTAL / norm) / jnp.sqrt(probability)
        for part, first, count, start, value in rows:
            f_ref[part, pl.ds(first, count), pl.ds(start, 128)] = value * scale
        p_ref[0] = jnp.max(probability)
        chosen_ref[0] = jnp.where(chosen == place.row, 1, 0) + jnp.where(p_ref[0] > 0.0, 0, 2)

    if shared:

        @pl.when(place.owner)
        def _():
            own.start()
            own.wait()
            wait_for(in_buf, 127 * 2, recv_sem.at[0])
            columns = []
            for block_of in range(2):
                b = in_buf[pl.ds(block_of, 128, stride=2), :]
                swapped = pltpu.roll(b, 64, axis=1)
                columns.append(
                    jnp.concatenate([b, jnp.where(first_half, -swapped, swapped)], axis=0)
                )
            psi = dot_split(top, split(jnp.concatenate(columns, axis=1)))
            norm = jnp.sum(psi * psi, axis=0, keepdims=True)
            picked = jnp.zeros((8, 256), F32)
            for group in range(16):
                picked = picked + jnp.where(chosen == group, psi[group * 8 : group * 8 + 8], 0.0)
            kept = jnp.sum(picked * picked, axis=0, keepdims=True)
            for block_of in range(2):
                back_out[pl.ds(block_of, 8, stride=3), :] = picked[
                    :, block_of * 128 : block_of * 128 + 128
                ]
            sums = fold(norm[:, :128] + norm[:, 128:], kept[:, :128] + kept[:, 128:])
            back_out[pl.ds(2, 8, stride=3), :] = jnp.broadcast_to(sums, (8, 128))
            pl.semaphore_wait(ready_sem, 64)
            each_other(send_back)
            own_back.start()
            own_back.wait()
            wait_for(back_in, 63 * 3, recv_sem.at[1])

        @pl.when(jnp.logical_not(place.owner))
        def _():
            wait_for(back_in, 64 * 3, recv_sem.at[1])

        finish(
            back_in[pl.ds(2, 64, stride=3), :],
            [(0, n * 64, 64, 0, back_in[pl.ds(n, 64, stride=3), :]) for n in range(2)],
        )

        @pl.when(place.owner)
        def _():
            wait_for(out_buf, 63 * 2, send_sem.at[0])
            wait_for(x_ref, 127 * 3, send_sem.at[1])

        @pl.when(jnp.logical_not(place.owner))
        def _():
            wait_for(out_buf, 64 * 2, send_sem.at[0])

        return

    own.wait()
    wait_for(in_buf, 127 * per_block, recv_sem.at[0])
    norm = jnp.zeros((1, 128), F32)
    kept = jnp.zeros((1, 128), F32)
    for g in range(groups):
        b = [in_buf[pl.ds(part * groups + g, 128, stride=per_block), :] for part in range(parts)]
        psi = dot_split(top, split(jnp.concatenate(b, axis=0)))
        norm = norm + jnp.sum(psi * psi, axis=0, keepdims=True)
        for part in range(parts):
            picked = jnp.zeros((8, 128), F32)
            for group in range(16):
                at = part * 128 + group * 8
                picked = picked + jnp.where(chosen == group, psi[at : at + 8], 0.0)
            kept = kept + jnp.sum(picked * picked, axis=0, keepdims=True)
            back_out[pl.ds(part * groups + g, 8, stride=per_back), :] = picked
    back_out[pl.ds(per_block, 8, stride=per_back), :] = jnp.broadcast_to(fold(norm, kept), (8, 128))
    each_other(send_back)
    own_back.start()
    own_back.wait()
    wait_for(back_in, 127 * per_back, recv_sem.at[1])
    finish(
        back_in[pl.ds(per_block, 128, stride=per_back), :],
        [
            (part, 0, 128, g * 128, back_in[pl.ds(part * groups + g, 128, stride=per_back), :])
            for part in range(parts)
            for g in range(groups)
        ],
    )
    wait_for(out_buf, 127 * per_block, send_sem.at[0])
    wait_for(back_in, 127 * per_back, send_sem.at[1])


def fill_rows(values, out_hbm, sems, first):
    copies = [
        pltpu.make_async_copy(
            values.at[pl.ds(0, 256)], out_hbm.at[pl.ds(first + n * 256, 256)], sems.at[n]
        )
        for n in range(4)
    ]
    for copy in copies:
        copy.start()
    for copy in copies:
        copy.wait()


def expand_kernel(
    level, chosen_ref, p_ref, f_ref, packed_ref, zeros_hbm, out_hbm, p_hbm, buf, sems
):
    shared, parts, groups, width = layout(level)
    each = 8 // groups
    p_copy = pltpu.make_async_copy(p_ref, p_hbm, sems.at[4])
    p_copy.start()
    state = chosen_ref[0]

    @pl.when(lax.rem(state, 2) == 1)
    def _():
        packed = packed_ref[...]
        copies = []
        for part in range(2):
            start = part * 64 if shared else 0
            tables = [
                onehot(jnp.where(packed >= 0, packed + start + u * width, -1)) for u in range(each)
            ]
            for g in range(groups):
                high, low = split(f_ref[part % parts, :, pl.ds(g * 128, 128)])
                for u, table in enumerate(tables):
                    q = g * each + u
                    buf[pl.ds(part * 1024 + q, 128, stride=8), :] = mm(high, table) + mm(low, table)
            here = pl.ds(part * 1024, 1024)
            copies.append(pltpu.make_async_copy(buf.at[here], out_hbm.at[here], sems.at[part]))
            copies[-1].start()
        for copy in copies:
            copy.wait()

    @pl.when(state == 0)
    def _():
        buf[pl.ds(0, 256), :] = jnp.zeros((256, 128), F32)
        fill_rows(buf, out_hbm, sems, 1024)

    @pl.when(state == 2)
    def _():
        buf[...] = jnp.full((2048, 128), jnp.nan, F32)
        copy = pltpu.make_async_copy(buf, out_hbm, sems.at[0])
        copy.start()
        copy.wait()

    p_copy.wait()


def run_level(level, buffer, x, local_gates, top_gates, placement, damping, branches, outcomes):
    shared, parts, groups, _ = layout(level)
    per_block = 2 if shared else parts * groups
    per_back = per_block + 1
    owners = 64 if shared else 128
    vmem = pl.BlockSpec(memory_space=pltpu.VMEM)
    hbm = pl.BlockSpec(memory_space=pltpu.HBM)
    smem = pl.BlockSpec(memory_space=pltpu.SMEM)
    packed, rows, chosen, probability = pl.pallas_call(
        functools.partial(main_kernel, level),
        out_shape=(
            pltpu.VMEM((parts, 128, 128 * groups), F32),
            pltpu.VMEM((1, 128), I32),
            pltpu.SMEM((1,), I32),
            pltpu.SMEM((1,), F32),
        ),
        in_specs=[hbm] * 7,
        out_specs=(vmem, vmem, smem, smem),
        scratch_shapes=[
            pltpu.VMEM((2048, 128), F32),
            pltpu.VMEM(local_gates.shape, F32),
            pltpu.VMEM(top_gates.shape, F32),
            pltpu.SMEM(placement.shape, I32),
            pltpu.SMEM(damping.shape, F32),
            pltpu.SMEM(branches.shape, I32),
            pltpu.SMEM(outcomes.shape, I32),
            pltpu.VMEM((owners * per_block, 128), F32),
            pltpu.VMEM((128 * per_block, 128), F32),
            pltpu.VMEM((8 * per_back, 128), F32),
            pltpu.VMEM((owners * per_back, 128), F32),
            pltpu.SemaphoreType.DMA((7,)),
            pltpu.SemaphoreType.DMA((2,)),
            pltpu.SemaphoreType.DMA((2,)),
            pltpu.SemaphoreType.DMA((2,)),
            pltpu.SemaphoreType.REGULAR,
        ],
        compiler_params=pltpu.CompilerParams(
            collective_id=level + 1, has_side_effects=True, vmem_limit_bytes=32 * 1024 * 1024
        ),
        name=f"window{level}",
    )(
        x,
        local_gates,
        top_gates,
        *(
            pltpu.with_memory_space_constraint(small, pltpu.HBM)
            for small in (placement, damping, branches, outcomes)
        ),
    )
    return pl.pallas_call(
        functools.partial(expand_kernel, level),
        out_shape=(
            pltpu.HBM((2048, 128), F32),
            pltpu.HBM((1,), F32),
        ),
        in_specs=[smem, smem, vmem, vmem, hbm],
        out_specs=(hbm, hbm),
        input_output_aliases={4: 0},
        scratch_shapes=[pltpu.VMEM((2048, 128), F32), pltpu.SemaphoreType.DMA((5,))],
        compiler_params=pltpu.CompilerParams(vmem_limit_bytes=32 * 1024 * 1024),
        name=f"expand{level}",
    )(
        chosen,
        probability,
        packed,
        rows,
        pltpu.with_memory_space_constraint(buffer, pltpu.HBM),
    )


def level_kernel(branches_hbm, *rest):
    *choice_refs, out_hbm, branches, zeros, sem, sems = rest
    load = pltpu.make_async_copy(branches_hbm, branches, sem)
    load.start()
    zeros[...] = jnp.zeros((256, 128), F32)
    fill_rows(zeros, out_hbm, sems, 0)
    load.wait()
    jumps = branches[0]
    for i in range(1, 7):
        jumps = jumps + branches[i]
    for limit, choice_ref in enumerate(choice_refs):
        choice_ref[0] = jnp.where(jumps > limit, 1, 0)


def choose_level(branches):
    return pl.pallas_call(
        level_kernel,
        out_shape=(pltpu.SMEM((1,), I32),) * 4 + (pltpu.HBM((2048, 128), F32),),
        in_specs=[pl.BlockSpec(memory_space=pltpu.HBM)],
        out_specs=(pl.BlockSpec(memory_space=pltpu.SMEM),) * 4
        + (pl.BlockSpec(memory_space=pltpu.HBM),),
        scratch_shapes=[
            pltpu.SMEM((7,), I32),
            pltpu.VMEM((256, 128), F32),
            pltpu.SemaphoreType.DMA,
            pltpu.SemaphoreType.DMA((4,)),
        ],
        name="level",
    )(branches)


def shards(initial_state, *small):
    *more, buffer = choose_level(small[4])
    level = [functools.partial(run_level, n) for n in range(5)]

    def either(choice, otherwise, then):
        return lambda choices, *args: lax.switch(
            choices[choice][0],
            [lambda _, *a: otherwise(*a), lambda _, *a: then(*a)],
            None,
            *args,
        )

    def two(choice, low, high):
        return lambda choices, *args: lax.switch(
            choices[choice][0],
            [lambda c, *a: low(c, *a), lambda c, *a: high(c, *a)],
            choices,
            *args,
        )

    tree = two(2, two(1, either(0, level[0], level[1]), lambda c, *a: level[2](*a)), either(3, level[3], level[4]))
    collapsed, probability = lax.optimization_barrier(
        tree(tuple(more), buffer, initial_state.reshape(2048, 128), *small)
    )
    return collapsed.reshape(initial_state.shape), probability.reshape(())


def solution(mesh):
    return jax.shard_map(
        shards,
        mesh=mesh,
        in_specs=(P(None, "gx", "gy", "gz", None), P(), P(), P(), P(), P(), P()),
        out_specs=(P(None, "gx", "gy", "gz", None), P()),
        check_vma=False,
    )
```

```python
import functools

import jax
import jax.numpy as jnp
from jax import lax
from jax.experimental import pallas as pl
from jax.experimental.pallas import tpu as pltpu
from jax.sharding import PartitionSpec as P

F32 = jnp.float32
BF16 = jnp.bfloat16
I32 = jnp.int32
MESH = pl.DeviceIdType.MESH
TOTAL = 16777216.0


def split(a):
    high = a.astype(BF16)
    return high, (a - high.astype(F32)).astype(BF16)


def mm(a, b, transposed=False):
    dims = (((1,), (1 if transposed else 0,)), ((), ()))
    return lax.dot_general(a, b, dims, preferred_element_type=F32)


def dot_split(a, b, transposed=False):
    return mm(a[0], b[0], transposed) + (mm(a[0], b[1], transposed) + mm(a[1], b[0], transposed))


def dot3(a, b, transposed=False):
    return dot_split(split(a), split(b), transposed)


def permuted_rows(onehot, b):
    high, low = split(b)
    return mm(onehot, high) + mm(onehot, low)


def permuted_columns(a, onehot):
    high, low = split(a)
    return mm(high, onehot) + mm(low, onehot)


def lanes(width=128):
    return lax.broadcasted_iota(I32, (1, width), 1)


def source(legs, k):
    out = jnp.zeros_like(k)
    for i in range(7):
        out = out | (((k >> legs[i]) & 1) << i)
    return out


def unsource(legs, s):
    out = jnp.zeros_like(s)
    for i in range(7):
        out = out | (((s >> i) & 1) << legs[i])
    return out


def hits(target, rows=128):
    return lax.broadcasted_iota(I32, (rows, target.shape[1]), 0) == target


def onehot(target, rows=128):
    return jnp.where(hits(target, rows), 1.0, 0.0).astype(BF16)


def compact_index(branches, j):
    out = jnp.zeros_like(j)
    count = jnp.int32(0)
    for i in range(7):
        stays = 1 - branches[i]
        out = out | ((((j >> i) & 1) * stays) << count)
        count = count + stays
    return out


def kraus_weight(branches, damping, j):
    weight = jnp.ones(j.shape, F32)
    for i in range(7):
        bit = ((j >> i) & 1) == 1
        d = jnp.full(j.shape, damping[i], F32)
        root = jnp.sqrt(jnp.where(branches[i] == 0, 1.0 - d, d))
        off = jnp.where(branches[i] == 0, 1.0, 0.0)
        weight = weight * jnp.where(bit, root, off)
    return weight


def complex_rows(pair):
    half = pair.shape[0] // 2
    r, i = pair[:half], pair[half:]
    return jnp.concatenate(
        [jnp.concatenate([r, -i], axis=1), jnp.concatenate([i, r], axis=1)], axis=0
    )


def complex_columns(pair):
    half = pair.shape[1] // 2
    r, i = pair[:, :half], pair[:, half:]
    return jnp.concatenate(
        [jnp.concatenate([r, i], axis=1), jnp.concatenate([-i, r], axis=1)], axis=0
    )


def side(gate_ref, which):
    return jnp.concatenate([gate_ref[which, 0], gate_ref[which, 1]], axis=1)


def stack_halves(pair):
    half = pair.shape[1] // 2
    return jnp.concatenate([pair[:, :half], pair[:, half:]], axis=0)


def side_halves(pair):
    half = pair.shape[0] // 2
    return jnp.concatenate([pair[:half], pair[half:]], axis=1)


HOPS = (0, 1, 2, 1)


def hops(offset):
    dy, dh, dz, dl = offset
    return HOPS[dy] + HOPS[dz] + (2 if (dh, dl) == (1, 0) else dh | dl)


CHIPS = [
    (dy, dh, dz, dl)
    for dy in range(4)
    for dh in range(2)
    for dz in range(4)
    for dl in range(2)
    if dy or dh or dz or dl
]
FAR = [sorted((o for o in CHIPS if hops(o) in at), key=hops, reverse=True) for at in ((6, 5), (4,))]
NEAR = [[o for o in CHIPS if hops(o) == at] for at in (3, 2, 1)]


def each_core(classes, act):
    for offsets in classes:

        @pl.loop(0, 2)
        def _(other, offsets=offsets):
            for offset in offsets:
                act(offset, other)


OWNERS = [
    (dy, dh, f, dl)
    for dy in range(4)
    for dh in range(2)
    for f in range(2)
    for dl in range(2)
    if dy or dh or f or dl
]
OWNER_CLASSES = [[o for o in OWNERS if hops(o) in at] for at in ((5,), (4,), (3,), (2,), (1,))]


def each_owner(place, act):
    each_core(OWNER_CLASSES, act)
    act((0, 0, 0, 0), 1)

    @pl.when(jnp.logical_not(place.owner))
    def _():
        act((0, 0, 0, 0), 0)


def each_other(act):
    each_core(FAR + NEAR, act)
    act((0, 0, 0, 0), 1)


class Place:
    def __init__(self):
        gx, gy, gz = (lax.axis_index(name) for name in ("gx", "gy", "gz"))
        self.index = (gx * 4 + gy) * 8 + gz
        self.row, self.column = gx * 4 + gy, gz
        self.core, xh = lax.rem(gy, 2), lax.div(gy, 2)
        z, xl = lax.div(gz, 2), lax.rem(gz, 2)
        self.ys = [gx] + [lax.rem(gx + d, 4) for d in (1, 2, 3)]
        zs = [z] + [lax.rem(z + d, 4) for d in (1, 2, 3)]
        self.owner = gz < 4
        self.owner_index = self.row * 4 + gz
        near = lax.div(lax.rem(z + 1, 4), 2)
        owner_zs = [near, 1 - near]
        self.xhs = [xh * 2, 2 - xh * 2]
        xls = [xl, 1 - xl]
        self.gzs = [[zs[dz] * 2 + xls[dl] for dl in range(2)] for dz in range(4)]
        self.owner_gzs = [[owner_zs[f] * 2 + xls[dl] for dl in range(2)] for f in range(2)]

    def device(self, offset, other):
        dy, dh, dz, dl = offset
        core = self.core + other * (1 - 2 * self.core)
        return (self.ys[dy], self.xhs[dh] + core, self.gzs[dz][dl])

    def owner_device(self, offset, other):
        dy, dh, f, dl = offset
        core = self.core + other * (1 - 2 * self.core)
        return (self.ys[dy], self.xhs[dh] + core, self.owner_gzs[f][dl])

    def column_of(self, offset):
        return self.gzs[offset[2]][offset[3]]

    def index_of(self, offset, other):
        gx, gy, gz = self.device(offset, other)
        return (gx * 4 + gy) * 8 + gz


def block(ref, index, rows):
    return ref.at[pl.ds(index * rows, rows)]


def wait_for(ref, rows, sem):
    part = ref.at[pl.ds(0, rows)]
    pltpu.make_async_copy(part, part, sem).wait()


def layout(level):
    shared = level > 3
    return shared, 1 if shared else 2, max(8 >> level, 1), 128 >> level


def main_kernel(
    level,
    x_hbm,
    local_hbm,
    top_hbm,
    placement_hbm,
    damping_hbm,
    branches_hbm,
    outcomes_hbm,
    f_ref,
    packed_ref,
    chosen_ref,
    p_ref,
    x_ref,
    local_ref,
    top_ref,
    placement,
    damping,
    branches,
    outcomes,
    out_buf,
    in_buf,
    back_out,
    back_in,
    in_sem,
    send_sem,
    recv_sem,
    own_sem,
    ready_sem,
):
    shared, parts, groups, width = layout(level)
    per_block = 2 if shared else parts * groups
    per_back = per_block + 1
    place = Place()

    barrier = pltpu.get_barrier_semaphore()

    def enter(offset, other):
        pl.semaphore_signal(
            barrier, inc=1, device_id=place.device(offset, other), device_id_type=MESH
        )

    if shared:
        pl.when(place.owner)(lambda: each_other(enter))
    else:
        each_core(FAR, enter)
    loads = [
        pltpu.make_async_copy(src, dst, in_sem.at[n])
        for n, (src, dst) in enumerate(
            (
                (branches_hbm, branches),
                (damping_hbm, damping),
                (placement_hbm, placement),
                (outcomes_hbm, outcomes),
                (local_hbm, local_ref),
                (x_hbm, x_ref),
                (top_hbm, top_ref),
            )
        )
    ]
    for load in loads:
        load.start()
    if not shared:
        each_core(NEAR, enter)
        enter((0, 0, 0, 0), 1)
    for load in loads[:6]:
        load.wait()

    legs = [[placement[t, i] for i in range(7)] for t in range(5)]
    branch = [branches[i] for i in range(7)]
    damp = [damping[i] for i in range(7)]
    lane = lanes()

    after = unsource(legs[3], lane)
    left = jnp.where(
        hits(compact_index(branch, after), width), kraus_weight(branch, damp, after), 0.0
    )
    left = dot3(left, side(local_ref, 2))
    right = permuted_rows(
        onehot(source(legs[3], unsource(legs[0], lane))), side(local_ref, 0)
    )
    right = permuted_columns(stack_halves(right), onehot(source(legs[0], lane)))
    low = stack_halves(dot3(left, complex_columns(side_halves(right))))
    low = split(complex_rows(low))

    middle = unsource(legs[1], lane)
    if shared:
        middle = ((middle >> 2) & 1) * 64 + (middle >> 3) * 4 + (middle & 3)
    mid = permuted_rows(onehot(middle), side(local_ref, 1))
    mid = permuted_columns(stack_halves(mid), onehot(source(legs[1], lane)))
    mid = complex_rows(mid)
    mid = split(mid[:128] if shared else mid)

    rows = jnp.concatenate(
        [
            jnp.concatenate(
                [x_ref[pl.ds(q, 128, stride=8), :], x_ref[pl.ds(1024 + q, 128, stride=8), :]], axis=1
            )
            for q in range(8)
        ],
        axis=0,
    )
    z = dot_split(low, split(rows), transposed=True)
    for g in range(groups):
        pieces, turned = [], []
        for u in range(8 // groups):
            q = g * (8 // groups) + u
            piece = z[:, q * 128 : q * 128 + 128]
            r, i = piece[:width], piece[width:]
            pieces.append(jnp.concatenate([r, i], axis=1))
            turned.append(jnp.concatenate([i, -r], axis=1))
        if shared:
            pieces = pieces + turned
        y = dot_split(mid, split(jnp.concatenate(pieces, axis=0)), transposed=True)
        if shared:
            for block_of in range(2):
                out_buf[pl.ds(block_of, 64, stride=2), :] = y[block_of * 64 : block_of * 64 + 64]
            continue
        for part in range(parts):
            out_buf[pl.ds(part * groups + g, 128, stride=per_block), :] = y[
                part * 128 : part * 128 + 128
            ]

    if shared:
        pl.when(place.owner)(lambda: pl.semaphore_wait(barrier, 63))
        pl.when(jnp.logical_not(place.owner))(lambda: pl.semaphore_wait(barrier, 64))
    else:
        pl.semaphore_wait(barrier, 127)

    def send(offset, other):
        pltpu.make_async_remote_copy(
            src_ref=block(out_buf, place.index_of(offset, other), per_block),
            dst_ref=block(in_buf, place.index, per_block),
            send_sem=send_sem.at[0],
            recv_sem=recv_sem.at[0],
            device_id=place.device(offset, other),
            device_id_type=MESH,
        ).start()

    slot = place.owner_index if shared else place.index
    own = pltpu.make_async_copy(
        block(out_buf, slot, per_block), block(in_buf, place.index, per_block), own_sem.at[0]
    )

    def send_owner(offset, other):
        gx, gy, gz = device = place.owner_device(offset, other)
        pltpu.make_async_remote_copy(
            src_ref=block(out_buf, (gx * 4 + gy) * 4 + gz, 2),
            dst_ref=block(in_buf, place.index, 2),
            send_sem=send_sem.at[0],
            recv_sem=recv_sem.at[0],
            device_id=device,
            device_id_type=MESH,
        ).start()

    def tell_owner(offset, other):
        pl.semaphore_signal(
            ready_sem, inc=1, device_id=place.owner_device(offset, other), device_id_type=MESH
        )

    if shared:
        each_owner(place, send_owner)
        pl.when(jnp.logical_not(place.owner))(lambda: each_owner(place, tell_owner))
    else:
        each_other(send)
        own.start()

    loads[6].wait()
    zero_row = jnp.zeros_like(lane)
    for n in range(7):
        zero_row = zero_row | (((lane >> n) & 1) * branch[n])
    packed_ref[...] = jnp.where(zero_row == 0, compact_index(branch, lane), -1)

    top = permuted_rows(onehot(unsource(legs[4], lane)), side(top_ref, 1))
    top = permuted_columns(
        stack_halves(top), onehot(source(legs[4], unsource(legs[2], lane)))
    )
    top = dot3(side_halves(top), complex_columns(side(top_ref, 0)))
    top = permuted_columns(stack_halves(top), onehot(source(legs[2], lane)))
    top = split(side_halves(top) if shared else complex_rows(top))
    chosen = outcomes[0] * 8 + outcomes[1] * 4 + outcomes[2] * 2 + outcomes[3]

    first_half = lane < 64

    def send_back(offset, other):
        pltpu.make_async_remote_copy(
            src_ref=block(back_out, place.column_of(offset), per_back),
            dst_ref=block(back_in, slot, per_back),
            send_sem=send_sem.at[1],
            recv_sem=recv_sem.at[1],
            device_id=place.device(offset, other),
            device_id_type=MESH,
        ).start()

    own_back = pltpu.make_async_copy(
        block(back_out, place.column, per_back), block(back_in, slot, per_back), own_sem.at[1]
    )

    def fold(norm, kept):
        return jnp.where(
            first_half, norm + pltpu.roll(norm, 64, axis=1), kept + pltpu.roll(kept, 64, axis=1)
        )

    def finish(sums, rows):
        sums = jnp.sum(sums, axis=0, keepdims=True)
        norm = jnp.sum(jnp.where(first_half, sums, 0.0), keepdims=True)
        kept = jnp.sum(jnp.where(first_half, 0.0, sums), keepdims=True)
        probability = kept / norm
        scale = jnp.sqrt(TOTAL / norm) / jnp.sqrt(probability)
        for part, first, count, start, value in rows:
            f_ref[part, pl.ds(first, count), pl.ds(start, 128)] = value * scale
        p_ref[0] = jnp.max(probability)
        chosen_ref[0] = jnp.where(chosen == place.row, 1, 0) + jnp.where(p_ref[0] > 0.0, 0, 2)

    if shared:

        @pl.when(place.owner)
        def _():
            own.start()
            own.wait()
            wait_for(in_buf, 127 * 2, recv_sem.at[0])
            columns = []
            for block_of in range(2):
                b = in_buf[pl.ds(block_of, 128, stride=2), :]
                swapped = pltpu.roll(b, 64, axis=1)
                columns.append(
                    jnp.concatenate([b, jnp.where(first_half, -swapped, swapped)], axis=0)
                )
            psi = dot_split(top, split(jnp.concatenate(columns, axis=1)))
            norm = jnp.sum(psi * psi, axis=0, keepdims=True)
            picked = jnp.zeros((8, 256), F32)
            for group in range(16):
                picked = picked + jnp.where(chosen == group, psi[group * 8 : group * 8 + 8], 0.0)
            kept = jnp.sum(picked * picked, axis=0, keepdims=True)
            for block_of in range(2):
                back_out[pl.ds(block_of, 8, stride=3), :] = picked[
                    :, block_of * 128 : block_of * 128 + 128
                ]
            sums = fold(norm[:, :128] + norm[:, 128:], kept[:, :128] + kept[:, 128:])
            back_out[pl.ds(2, 8, stride=3), :] = jnp.broadcast_to(sums, (8, 128))
            pl.semaphore_wait(ready_sem, 64)
            each_other(send_back)
            own_back.start()
            own_back.wait()
            wait_for(back_in, 63 * 3, recv_sem.at[1])

        @pl.when(jnp.logical_not(place.owner))
        def _():
            wait_for(back_in, 64 * 3, recv_sem.at[1])

        finish(
            back_in[pl.ds(2, 64, stride=3), :],
            [(0, n * 64, 64, 0, back_in[pl.ds(n, 64, stride=3), :]) for n in range(2)],
        )

        @pl.when(place.owner)
        def _():
            wait_for(out_buf, 63 * 2, send_sem.at[0])
            wait_for(x_ref, 127 * 3, send_sem.at[1])

        @pl.when(jnp.logical_not(place.owner))
        def _():
            wait_for(out_buf, 64 * 2, send_sem.at[0])

        return

    own.wait()
    wait_for(in_buf, 127 * per_block, recv_sem.at[0])
    norm = jnp.zeros((1, 128), F32)
    kept = jnp.zeros((1, 128), F32)
    for g in range(groups):
        b = [in_buf[pl.ds(part * groups + g, 128, stride=per_block), :] for part in range(parts)]
        psi = dot_split(top, split(jnp.concatenate(b, axis=0)))
        norm = norm + jnp.sum(psi * psi, axis=0, keepdims=True)
        for part in range(parts):
            picked = jnp.zeros((8, 128), F32)
            for group in range(16):
                at = part * 128 + group * 8
                picked = picked + jnp.where(chosen == group, psi[at : at + 8], 0.0)
            kept = kept + jnp.sum(picked * picked, axis=0, keepdims=True)
            back_out[pl.ds(part * groups + g, 8, stride=per_back), :] = picked
    back_out[pl.ds(per_block, 8, stride=per_back), :] = jnp.broadcast_to(fold(norm, kept), (8, 128))
    each_other(send_back)
    own_back.start()
    own_back.wait()
    wait_for(back_in, 127 * per_back, recv_sem.at[1])
    finish(
        back_in[pl.ds(per_block, 128, stride=per_back), :],
        [
            (part, 0, 128, g * 128, back_in[pl.ds(part * groups + g, 128, stride=per_back), :])
            for part in range(parts)
            for g in range(groups)
        ],
    )
    wait_for(out_buf, 127 * per_block, send_sem.at[0])
    wait_for(back_in, 127 * per_back, send_sem.at[1])


def fill_rows(values, out_hbm, sems, first):
    copies = [
        pltpu.make_async_copy(
            values.at[pl.ds(0, 256)], out_hbm.at[pl.ds(first + n * 256, 256)], sems.at[n]
        )
        for n in range(4)
    ]
    for copy in copies:
        copy.start()
    for copy in copies:
        copy.wait()


def expand_kernel(
    level, chosen_ref, p_ref, f_ref, packed_ref, zeros_hbm, out_hbm, p_hbm, buf, sems
):
    shared, parts, groups, width = layout(level)
    each = 8 // groups
    p_copy = pltpu.make_async_copy(p_ref, p_hbm, sems.at[4])
    p_copy.start()
    state = chosen_ref[0]

    @pl.when(lax.rem(state, 2) == 1)
    def _():
        packed = packed_ref[...]
        copies = []
        for part in range(2):
            start = part * 64 if shared else 0
            tables = [
                onehot(jnp.where(packed >= 0, packed + start + u * width, -1)) for u in range(each)
            ]
            for g in range(groups):
                high, low = split(f_ref[part % parts, :, pl.ds(g * 128, 128)])
                if shared:
                    lane = lanes()
                    owner = lane & 63
                    order = onehot((owner >> 2) * 8 + (lane >> 6) * 4 + (owner & 3))
                    high, low = mm(order, high).astype(BF16), mm(order, low).astype(BF16)
                for u, table in enumerate(tables):
                    q = g * each + u
                    buf[pl.ds(part * 1024 + q, 128, stride=8), :] = mm(high, table) + mm(low, table)
            here = pl.ds(part * 1024, 1024)
            copies.append(pltpu.make_async_copy(buf.at[here], out_hbm.at[here], sems.at[part]))
            copies[-1].start()
        for copy in copies:
            copy.wait()

    @pl.when(state == 0)
    def _():
        buf[pl.ds(0, 256), :] = jnp.zeros((256, 128), F32)
        fill_rows(buf, out_hbm, sems, 1024)

    @pl.when(state == 2)
    def _():
        buf[...] = jnp.full((2048, 128), jnp.nan, F32)
        copy = pltpu.make_async_copy(buf, out_hbm, sems.at[0])
        copy.start()
        copy.wait()

    p_copy.wait()


def run_level(level, buffer, x, local_gates, top_gates, placement, damping, branches, outcomes):
    shared, parts, groups, _ = layout(level)
    per_block = 2 if shared else parts * groups
    per_back = per_block + 1
    owners = 64 if shared else 128
    vmem = pl.BlockSpec(memory_space=pltpu.VMEM)
    hbm = pl.BlockSpec(memory_space=pltpu.HBM)
    smem = pl.BlockSpec(memory_space=pltpu.SMEM)
    packed, rows, chosen, probability = pl.pallas_call(
        functools.partial(main_kernel, level),
        out_shape=(
            pltpu.VMEM((parts, 128, 128 * groups), F32),
            pltpu.VMEM((1, 128), I32),
            pltpu.SMEM((1,), I32),
            pltpu.SMEM((1,), F32),
        ),
        in_specs=[hbm] * 7,
        out_specs=(vmem, vmem, smem, smem),
        scratch_shapes=[
            pltpu.VMEM((2048, 128), F32),
            pltpu.VMEM(local_gates.shape, F32),
            pltpu.VMEM(top_gates.shape, F32),
            pltpu.SMEM(placement.shape, I32),
            pltpu.SMEM(damping.shape, F32),
            pltpu.SMEM(branches.shape, I32),
            pltpu.SMEM(outcomes.shape, I32),
            pltpu.VMEM((owners * per_block, 128), F32),
            pltpu.VMEM((128 * per_block, 128), F32),
            pltpu.VMEM((8 * per_back, 128), F32),
            pltpu.VMEM((owners * per_back, 128), F32),
            pltpu.SemaphoreType.DMA((7,)),
            pltpu.SemaphoreType.DMA((2,)),
            pltpu.SemaphoreType.DMA((2,)),
            pltpu.SemaphoreType.DMA((2,)),
            pltpu.SemaphoreType.REGULAR,
        ],
        compiler_params=pltpu.CompilerParams(
            collective_id=level + 1, has_side_effects=True, vmem_limit_bytes=32 * 1024 * 1024
        ),
        name=f"window{level}",
    )(
        x,
        local_gates,
        top_gates,
        *(
            pltpu.with_memory_space_constraint(small, pltpu.HBM)
            for small in (placement, damping, branches, outcomes)
        ),
    )
    return pl.pallas_call(
        functools.partial(expand_kernel, level),
        out_shape=(
            pltpu.HBM((2048, 128), F32),
            pltpu.HBM((1,), F32),
        ),
        in_specs=[smem, smem, vmem, vmem, hbm],
        out_specs=(hbm, hbm),
        input_output_aliases={4: 0},
        scratch_shapes=[pltpu.VMEM((2048, 128), F32), pltpu.SemaphoreType.DMA((5,))],
        compiler_params=pltpu.CompilerParams(vmem_limit_bytes=32 * 1024 * 1024),
        name=f"expand{level}",
    )(
        chosen,
        probability,
        packed,
        rows,
        pltpu.with_memory_space_constraint(buffer, pltpu.HBM),
    )


def level_kernel(branches_hbm, *rest):
    *choice_refs, out_hbm, branches, zeros, sem, sems = rest
    load = pltpu.make_async_copy(branches_hbm, branches, sem)
    load.start()
    zeros[...] = jnp.zeros((256, 128), F32)
    fill_rows(zeros, out_hbm, sems, 0)
    load.wait()
    jumps = branches[0]
    for i in range(1, 7):
        jumps = jumps + branches[i]
    for limit, choice_ref in enumerate(choice_refs):
        choice_ref[0] = jnp.where(jumps > limit, 1, 0)


def choose_level(branches):
    return pl.pallas_call(
        level_kernel,
        out_shape=(pltpu.SMEM((1,), I32),) * 4 + (pltpu.HBM((2048, 128), F32),),
        in_specs=[pl.BlockSpec(memory_space=pltpu.HBM)],
        out_specs=(pl.BlockSpec(memory_space=pltpu.SMEM),) * 4
        + (pl.BlockSpec(memory_space=pltpu.HBM),),
        scratch_shapes=[
            pltpu.SMEM((7,), I32),
            pltpu.VMEM((256, 128), F32),
            pltpu.SemaphoreType.DMA,
            pltpu.SemaphoreType.DMA((4,)),
        ],
        name="level",
    )(branches)


def shards(initial_state, *small):
    *more, buffer = choose_level(small[4])
    level = [functools.partial(run_level, n) for n in range(5)]

    def either(choice, otherwise, then):
        return lambda choices, *args: lax.switch(
            choices[choice][0],
            [lambda _, *a: otherwise(*a), lambda _, *a: then(*a)],
            None,
            *args,
        )

    def two(choice, low, high):
        return lambda choices, *args: lax.switch(
            choices[choice][0],
            [lambda c, *a: low(c, *a), lambda c, *a: high(c, *a)],
            choices,
            *args,
        )

    tree = two(2, two(1, either(0, level[0], level[1]), lambda c, *a: level[2](*a)), either(3, level[3], level[4]))
    collapsed, probability = lax.optimization_barrier(
        tree(tuple(more), buffer, initial_state.reshape(2048, 128), *small)
    )
    return collapsed.reshape(initial_state.shape), probability.reshape(())


def solution(mesh):
    return jax.shard_map(
        shards,
        mesh=mesh,
        in_specs=(P(None, "gx", "gy", "gz", None), P(), P(), P(), P(), P(), P()),
        out_specs=(P(None, "gx", "gy", "gz", None), P()),
        check_vma=False,
    )
```

```python
import functools

import jax
import jax.numpy as jnp
from jax import lax
from jax.experimental import pallas as pl
from jax.experimental.pallas import tpu as pltpu
from jax.sharding import PartitionSpec as P

F32 = jnp.float32
BF16 = jnp.bfloat16
I32 = jnp.int32
MESH = pl.DeviceIdType.MESH
TOTAL = 16777216.0


def split(a):
    high = a.astype(BF16)
    return high, (a - high.astype(F32)).astype(BF16)


def mm(a, b, transposed=False):
    dims = (((1,), (1 if transposed else 0,)), ((), ()))
    return lax.dot_general(a, b, dims, preferred_element_type=F32)


def dot_split(a, b, transposed=False):
    return mm(a[0], b[0], transposed) + (mm(a[0], b[1], transposed) + mm(a[1], b[0], transposed))


def dot3(a, b, transposed=False):
    return dot_split(split(a), split(b), transposed)


def permuted_rows(onehot, b):
    high, low = split(b)
    return mm(onehot, high) + mm(onehot, low)


def permuted_columns(a, onehot):
    high, low = split(a)
    return mm(high, onehot) + mm(low, onehot)


def lanes(width=128):
    return lax.broadcasted_iota(I32, (1, width), 1)


def source(legs, k):
    out = jnp.zeros_like(k)
    for i in range(7):
        out = out | (((k >> legs[i]) & 1) << i)
    return out


def unsource(legs, s):
    out = jnp.zeros_like(s)
    for i in range(7):
        out = out | (((s >> i) & 1) << legs[i])
    return out


def hits(target, rows=128):
    return lax.broadcasted_iota(I32, (rows, target.shape[1]), 0) == target


def onehot(target, rows=128):
    return jnp.where(hits(target, rows), 1.0, 0.0).astype(BF16)


def compact_index(branches, j):
    out = jnp.zeros_like(j)
    count = jnp.int32(0)
    for i in range(7):
        stays = 1 - branches[i]
        out = out | ((((j >> i) & 1) * stays) << count)
        count = count + stays
    return out


def kraus_weight(branches, damping, j):
    weight = jnp.ones(j.shape, F32)
    for i in range(7):
        bit = ((j >> i) & 1) == 1
        d = jnp.full(j.shape, damping[i], F32)
        root = jnp.sqrt(jnp.where(branches[i] == 0, 1.0 - d, d))
        off = jnp.where(branches[i] == 0, 1.0, 0.0)
        weight = weight * jnp.where(bit, root, off)
    return weight


def complex_rows(pair):
    half = pair.shape[0] // 2
    r, i = pair[:half], pair[half:]
    return jnp.concatenate(
        [jnp.concatenate([r, -i], axis=1), jnp.concatenate([i, r], axis=1)], axis=0
    )


def complex_columns(pair):
    half = pair.shape[1] // 2
    r, i = pair[:, :half], pair[:, half:]
    return jnp.concatenate(
        [jnp.concatenate([r, i], axis=1), jnp.concatenate([-i, r], axis=1)], axis=0
    )


def side(gate_ref, which):
    return jnp.concatenate([gate_ref[which, 0], gate_ref[which, 1]], axis=1)


def stack_halves(pair):
    half = pair.shape[1] // 2
    return jnp.concatenate([pair[:, :half], pair[:, half:]], axis=0)


def side_halves(pair):
    half = pair.shape[0] // 2
    return jnp.concatenate([pair[:half], pair[half:]], axis=1)


HOPS = (0, 1, 2, 1)


def hops(offset):
    dy, dh, dz, dl = offset
    return HOPS[dy] + HOPS[dz] + (2 if (dh, dl) == (1, 0) else dh | dl)


CHIPS = [
    (dy, dh, dz, dl)
    for dy in range(4)
    for dh in range(2)
    for dz in range(4)
    for dl in range(2)
    if dy or dh or dz or dl
]
FAR = [sorted((o for o in CHIPS if hops(o) in at), key=hops, reverse=True) for at in ((6, 5), (4,))]
NEAR = [[o for o in CHIPS if hops(o) == at] for at in (3, 2, 1)]


def each_core(classes, act):
    for offsets in classes:

        @pl.loop(0, 2)
        def _(other, offsets=offsets):
            for offset in offsets:
                act(offset, other)


OWNERS = [
    (dy, dh, f, dl)
    for dy in range(4)
    for dh in range(2)
    for f in range(2)
    for dl in range(2)
    if dy or dh or f or dl
]
OWNER_CLASSES = [[o for o in OWNERS if hops(o) in at] for at in ((5,), (4,), (3,), (2,), (1,))]


def each_owner(place, act):
    each_core(OWNER_CLASSES, act)
    act((0, 0, 0, 0), 1)

    @pl.when(jnp.logical_not(place.owner))
    def _():
        act((0, 0, 0, 0), 0)


def each_other(act):
    each_core(FAR + NEAR, act)
    act((0, 0, 0, 0), 1)


class Place:
    def __init__(self):
        gx, gy, gz = (lax.axis_index(name) for name in ("gx", "gy", "gz"))
        self.index = (gx * 4 + gy) * 8 + gz
        self.row, self.column = gx * 4 + gy, gz
        self.core, xh = lax.rem(gy, 2), lax.div(gy, 2)
        z, xl = lax.div(gz, 2), lax.rem(gz, 2)
        self.ys = [gx] + [lax.rem(gx + d, 4) for d in (1, 2, 3)]
        zs = [z] + [lax.rem(z + d, 4) for d in (1, 2, 3)]
        self.owner = gz < 4
        self.owner_index = self.row * 4 + gz
        near = lax.div(lax.rem(z + 1, 4), 2)
        owner_zs = [near, 1 - near]
        self.xhs = [xh * 2, 2 - xh * 2]
        xls = [xl, 1 - xl]
        self.gzs = [[zs[dz] * 2 + xls[dl] for dl in range(2)] for dz in range(4)]
        self.owner_gzs = [[owner_zs[f] * 2 + xls[dl] for dl in range(2)] for f in range(2)]

    def device(self, offset, other):
        dy, dh, dz, dl = offset
        core = self.core + other * (1 - 2 * self.core)
        return (self.ys[dy], self.xhs[dh] + core, self.gzs[dz][dl])

    def owner_device(self, offset, other):
        dy, dh, f, dl = offset
        core = self.core + other * (1 - 2 * self.core)
        return (self.ys[dy], self.xhs[dh] + core, self.owner_gzs[f][dl])

    def column_of(self, offset):
        return self.gzs[offset[2]][offset[3]]

    def index_of(self, offset, other):
        gx, gy, gz = self.device(offset, other)
        return (gx * 4 + gy) * 8 + gz


def block(ref, index, rows):
    return ref.at[pl.ds(index * rows, rows)]


def wait_for(ref, rows, sem):
    part = ref.at[pl.ds(0, rows)]
    pltpu.make_async_copy(part, part, sem).wait()


def layout(level):
    shared = level > 3
    return shared, 1 if shared else 2, max(8 >> level, 1), 128 >> level


def main_kernel(
    level,
    match,
    x_hbm,
    local_hbm,
    top_hbm,
    placement_hbm,
    damping_hbm,
    branches_hbm,
    outcomes_hbm,
    f_ref,
    packed_ref,
    chosen_ref,
    p_ref,
    x_ref,
    local_ref,
    top_ref,
    placement,
    damping,
    branches,
    outcomes,
    out_buf,
    in_buf,
    back_out,
    back_in,
    sums_in,
    in_sem,
    send_sem,
    recv_sem,
    own_sem,
    ready_sem,
):
    shared, parts, groups, width = layout(level)
    per_block = 2 if shared else parts * groups
    per_back = per_block + 1
    place = Place()

    barrier = pltpu.get_barrier_semaphore()

    def enter(offset, other):
        pl.semaphore_signal(
            barrier, inc=1, device_id=place.device(offset, other), device_id_type=MESH
        )

    if shared:
        pl.when(place.owner)(lambda: each_other(enter))
    else:
        each_core(FAR, enter)
    loads = [
        pltpu.make_async_copy(src, dst, in_sem.at[n])
        for n, (src, dst) in enumerate(
            (
                (branches_hbm, branches),
                (damping_hbm, damping),
                (placement_hbm, placement),
                (outcomes_hbm, outcomes),
                (local_hbm, local_ref),
                (x_hbm, x_ref),
                (top_hbm, top_ref),
            )
        )
    ]
    for load in loads:
        load.start()
    if not shared:
        each_core(NEAR, enter)
        enter((0, 0, 0, 0), 1)
    for load in loads[:5]:
        load.wait()

    legs = [[placement[t, i] for i in range(7)] for t in range(5)]
    branch = [branches[i] for i in range(7)]
    damp = [damping[i] for i in range(7)]
    lane = lanes()

    after = unsource(legs[3], lane)
    left = jnp.where(
        hits(compact_index(branch, after), width), kraus_weight(branch, damp, after), 0.0
    )
    left = dot3(left, side(local_ref, 2))
    right = permuted_rows(
        onehot(source(legs[3], unsource(legs[0], lane))), side(local_ref, 0)
    )
    right = permuted_columns(stack_halves(right), onehot(source(legs[0], lane)))
    low = stack_halves(dot3(left, complex_columns(side_halves(right))))
    low = split(complex_rows(low))

    middle = unsource(legs[1], lane)
    if shared:
        middle = ((middle >> 2) & 1) * 64 + (middle >> 3) * 4 + (middle & 3)
    mid = permuted_rows(onehot(middle), side(local_ref, 1))
    mid = permuted_columns(stack_halves(mid), onehot(source(legs[1], lane)))
    mid = complex_rows(mid)
    mid = split(mid[:128] if shared else mid)

    loads[5].wait()
    rows = jnp.concatenate(
        [
            jnp.concatenate(
                [x_ref[pl.ds(q, 128, stride=8), :], x_ref[pl.ds(1024 + q, 128, stride=8), :]], axis=1
            )
            for q in range(8)
        ],
        axis=0,
    )
    z = dot_split(low, split(rows), transposed=True)
    for g in range(groups):
        pieces, turned = [], []
        for u in range(8 // groups):
            q = g * (8 // groups) + u
            piece = z[:, q * 128 : q * 128 + 128]
            r, i = piece[:width], piece[width:]
            pieces.append(jnp.concatenate([r, i], axis=1))
            turned.append(jnp.concatenate([i, -r], axis=1))
        if shared:
            pieces = pieces + turned
        y = dot_split(mid, split(jnp.concatenate(pieces, axis=0)), transposed=True)
        if shared:
            for block_of in range(2):
                out_buf[pl.ds(block_of, 64, stride=2), :] = y[block_of * 64 : block_of * 64 + 64]
            continue
        for part in range(parts):
            out_buf[pl.ds(part * groups + g, 128, stride=per_block), :] = y[
                part * 128 : part * 128 + 128
            ]

    if shared:
        pl.when(place.owner)(lambda: pl.semaphore_wait(barrier, 63))
        pl.when(jnp.logical_not(place.owner))(lambda: pl.semaphore_wait(barrier, 64))
    else:
        pl.semaphore_wait(barrier, 127)

    def send(offset, other):
        pltpu.make_async_remote_copy(
            src_ref=block(out_buf, place.index_of(offset, other), per_block),
            dst_ref=block(in_buf, place.index, per_block),
            send_sem=send_sem.at[0],
            recv_sem=recv_sem.at[0],
            device_id=place.device(offset, other),
            device_id_type=MESH,
        ).start()

    slot = place.owner_index if shared else place.index
    own = pltpu.make_async_copy(
        block(out_buf, slot, per_block), block(in_buf, place.index, per_block), own_sem.at[0]
    )

    def send_owner(offset, other):
        gx, gy, gz = device = place.owner_device(offset, other)
        pltpu.make_async_remote_copy(
            src_ref=block(out_buf, (gx * 4 + gy) * 4 + gz, 2),
            dst_ref=block(in_buf, place.index, 2),
            send_sem=send_sem.at[0],
            recv_sem=recv_sem.at[0],
            device_id=device,
            device_id_type=MESH,
        ).start()

    def tell_owner(offset, other):
        pl.semaphore_signal(
            ready_sem, inc=1, device_id=place.owner_device(offset, other), device_id_type=MESH
        )

    if shared:
        each_owner(place, send_owner)
        pl.when(jnp.logical_not(place.owner))(lambda: each_owner(place, tell_owner))
    else:
        each_other(send)
        own.start()

    loads[6].wait()
    zero_row = jnp.zeros_like(lane)
    for n in range(7):
        zero_row = zero_row | (((lane >> n) & 1) * branch[n])
    packed_ref[...] = jnp.where(zero_row == 0, compact_index(branch, lane), -1)

    top = permuted_rows(onehot(unsource(legs[4], lane)), side(top_ref, 1))
    top = permuted_columns(
        stack_halves(top), onehot(source(legs[4], unsource(legs[2], lane)))
    )
    top = dot3(side_halves(top), complex_columns(side(top_ref, 0)))
    top = permuted_columns(stack_halves(top), onehot(source(legs[2], lane)))
    top = split(side_halves(top) if shared else complex_rows(top))
    chosen = outcomes[0] * 8 + outcomes[1] * 4 + outcomes[2] * 2 + outcomes[3]

    first_half = lane < 64

    def send_back(offset, other):
        pltpu.make_async_remote_copy(
            src_ref=block(back_out, place.column_of(offset), per_back),
            dst_ref=block(back_in, slot, per_back),
            send_sem=send_sem.at[1],
            recv_sem=recv_sem.at[1],
            device_id=place.device(offset, other),
            device_id_type=MESH,
        ).start()

    own_back = pltpu.make_async_copy(
        block(back_out, place.column, per_back), block(back_in, slot, per_back), own_sem.at[1]
    )

    total_row = back_out.at[pl.ds(per_block, 1)]
    matches = [lax.div(y, 2) == (0 if match is None else match) for y in place.ys]

    def send_sums(offset, other):
        pltpu.make_async_remote_copy(
            src_ref=total_row,
            dst_ref=block(sums_in, slot, 1),
            send_sem=send_sem.at[2],
            recv_sem=recv_sem.at[2],
            device_id=place.device(offset, other),
            device_id_type=MESH,
        ).start()

    def to_both(dy, act):
        pl.when(matches[dy])(functools.partial(act, send_back))
        pl.when(jnp.logical_not(matches[dy]))(functools.partial(act, send_sums))

    def fold(norm, kept):
        return jnp.where(
            first_half, norm + pltpu.roll(norm, 64, axis=1), kept + pltpu.roll(kept, 64, axis=1)
        )

    def finish(sums, rows):
        sums = jnp.sum(sums, axis=0, keepdims=True)
        norm = jnp.sum(jnp.where(first_half, sums, 0.0), keepdims=True)
        kept = jnp.sum(jnp.where(first_half, 0.0, sums), keepdims=True)
        probability = kept / norm
        scale = jnp.sqrt(TOTAL / norm) / jnp.sqrt(probability)
        for part, first, count, start, value in rows:
            f_ref[part, pl.ds(first, count), pl.ds(start, 128)] = value * scale
        p_ref[0] = jnp.max(probability)
        chosen_ref[0] = jnp.where(chosen == place.row, 1, 0) + jnp.where(p_ref[0] > 0.0, 0, 2)

    if shared:

        @pl.when(place.owner)
        def _():
            own.start()
            own.wait()
            wait_for(in_buf, 127 * 2, recv_sem.at[0])
            columns = []
            for block_of in range(2):
                b = in_buf[pl.ds(block_of, 128, stride=2), :]
                swapped = pltpu.roll(b, 64, axis=1)
                columns.append(
                    jnp.concatenate([b, jnp.where(first_half, -swapped, swapped)], axis=0)
                )
            psi = dot_split(top, split(jnp.concatenate(columns, axis=1)))
            norm = jnp.sum(psi * psi, axis=0, keepdims=True)
            picked = jnp.zeros((8, 256), F32)
            for group in range(16):
                picked = picked + jnp.where(chosen == group, psi[group * 8 : group * 8 + 8], 0.0)
            kept = jnp.sum(picked * picked, axis=0, keepdims=True)
            for block_of in range(2):
                back_out[pl.ds(block_of, 8, stride=3), :] = picked[
                    :, block_of * 128 : block_of * 128 + 128
                ]
            sums = fold(norm[:, :128] + norm[:, 128:], kept[:, :128] + kept[:, 128:])
            back_out[pl.ds(2, 8, stride=3), :] = jnp.broadcast_to(sums, (8, 128))
            pl.semaphore_wait(ready_sem, 64)
            for offsets in FAR + NEAR:
                for dy in (2, 1, 3, 0):
                    group = [o for o in offsets if o[0] == dy]
                    if group:
                        to_both(dy, functools.partial(each_core, [group]))
            to_both(0, lambda act: act((0, 0, 0, 0), 1))

            @pl.when(matches[0])
            def _():
                own_back.start()
                own_back.wait()
                wait_for(back_in, 63 * 3, recv_sem.at[1])

            @pl.when(jnp.logical_not(matches[0]))
            def _():
                own_sums = pltpu.make_async_copy(total_row, block(sums_in, slot, 1), own_sem.at[1])
                own_sums.start()
                own_sums.wait()
                wait_for(sums_in, 63, recv_sem.at[2])

        @pl.when(jnp.logical_not(place.owner))
        def _():
            pl.when(matches[0])(lambda: wait_for(back_in, 64 * 3, recv_sem.at[1]))
            pl.when(jnp.logical_not(matches[0]))(lambda: wait_for(sums_in, 64, recv_sem.at[2]))

        @pl.when(matches[0])
        def _():
            finish(
                back_in[pl.ds(2, 64, stride=3), :],
                [(0, n * 64, 64, 0, back_in[pl.ds(n, 64, stride=3), :]) for n in range(2)],
            )

        @pl.when(jnp.logical_not(matches[0]))
        def _():
            finish(sums_in[...], [])

        @pl.when(place.owner)
        def _():
            wait_for(out_buf, 63 * 2, send_sem.at[0])

            @pl.when(matches[0])
            def _():
                wait_for(x_ref, 63 * 3, send_sem.at[1])
                wait_for(x_ref, 64, send_sem.at[2])

            @pl.when(jnp.logical_not(matches[0]))
            def _():
                wait_for(x_ref, 64 * 3, send_sem.at[1])
                wait_for(x_ref, 63, send_sem.at[2])

        @pl.when(jnp.logical_not(place.owner))
        def _():
            wait_for(out_buf, 64 * 2, send_sem.at[0])

        return

    own.wait()
    wait_for(in_buf, 127 * per_block, recv_sem.at[0])
    norm = jnp.zeros((1, 128), F32)
    kept = jnp.zeros((1, 128), F32)
    for g in range(groups):
        b = [in_buf[pl.ds(part * groups + g, 128, stride=per_block), :] for part in range(parts)]
        psi = dot_split(top, split(jnp.concatenate(b, axis=0)))
        norm = norm + jnp.sum(psi * psi, axis=0, keepdims=True)
        for part in range(parts):
            picked = jnp.zeros((8, 128), F32)
            for group in range(16):
                at = part * 128 + group * 8
                picked = picked + jnp.where(chosen == group, psi[at : at + 8], 0.0)
            kept = kept + jnp.sum(picked * picked, axis=0, keepdims=True)
            back_out[pl.ds(part * groups + g, 8, stride=per_back), :] = picked
    back_out[pl.ds(per_block, 8, stride=per_back), :] = jnp.broadcast_to(fold(norm, kept), (8, 128))
    each_other(send_back)
    own_back.start()
    own_back.wait()
    wait_for(back_in, 127 * per_back, recv_sem.at[1])
    finish(
        back_in[pl.ds(per_block, 128, stride=per_back), :],
        [
            (part, 0, 128, g * 128, back_in[pl.ds(part * groups + g, 128, stride=per_back), :])
            for part in range(parts)
            for g in range(groups)
        ],
    )
    wait_for(out_buf, 127 * per_block, send_sem.at[0])
    wait_for(back_in, 127 * per_back, send_sem.at[1])


def fill_rows(values, out_hbm, sems, first):
    copies = [
        pltpu.make_async_copy(
            values.at[pl.ds(0, 256)], out_hbm.at[pl.ds(first + n * 256, 256)], sems.at[n]
        )
        for n in range(4)
    ]
    for copy in copies:
        copy.start()
    for copy in copies:
        copy.wait()


def expand_kernel(
    level, chosen_ref, p_ref, f_ref, packed_ref, zeros_hbm, out_hbm, p_hbm, buf, sems
):
    shared, parts, groups, width = layout(level)
    each = 8 // groups
    p_copy = pltpu.make_async_copy(p_ref, p_hbm, sems.at[4])
    p_copy.start()
    state = chosen_ref[0]

    @pl.when(lax.rem(state, 2) == 1)
    def _():
        packed = packed_ref[...]
        copies = []
        for part in range(2):
            start = part * 64 if shared else 0
            tables = [
                onehot(jnp.where(packed >= 0, packed + start + u * width, -1)) for u in range(each)
            ]
            for g in range(groups):
                high, low = split(f_ref[part % parts, :, pl.ds(g * 128, 128)])
                if shared:
                    lane = lanes()
                    owner = lane & 63
                    order = onehot((owner >> 2) * 8 + (lane >> 6) * 4 + (owner & 3))
                    high, low = mm(order, high).astype(BF16), mm(order, low).astype(BF16)
                for u, table in enumerate(tables):
                    q = g * each + u
                    buf[pl.ds(part * 1024 + q, 128, stride=8), :] = mm(high, table) + mm(low, table)
            here = pl.ds(part * 1024, 1024)
            copies.append(pltpu.make_async_copy(buf.at[here], out_hbm.at[here], sems.at[part]))
            copies[-1].start()
        for copy in copies:
            copy.wait()

    @pl.when(state == 0)
    def _():
        buf[pl.ds(0, 256), :] = jnp.zeros((256, 128), F32)
        fill_rows(buf, out_hbm, sems, 1024)

    @pl.when(state == 2)
    def _():
        buf[...] = jnp.full((2048, 128), jnp.nan, F32)
        copy = pltpu.make_async_copy(buf, out_hbm, sems.at[0])
        copy.start()
        copy.wait()

    p_copy.wait()


KERNELS = ((0, None), (1, None), (2, None), (3, None), (4, 0), (4, 1))


def run_level(level, match, buffer, x, local_gates, top_gates, placement, damping, branches, outcomes):
    shared, parts, groups, _ = layout(level)
    per_block = 2 if shared else parts * groups
    per_back = per_block + 1
    owners = 64 if shared else 128
    vmem = pl.BlockSpec(memory_space=pltpu.VMEM)
    hbm = pl.BlockSpec(memory_space=pltpu.HBM)
    smem = pl.BlockSpec(memory_space=pltpu.SMEM)
    packed, rows, chosen, probability = pl.pallas_call(
        functools.partial(main_kernel, level, match),
        out_shape=(
            pltpu.VMEM((parts, 128, 128 * groups), F32),
            pltpu.VMEM((1, 128), I32),
            pltpu.SMEM((1,), I32),
            pltpu.SMEM((1,), F32),
        ),
        in_specs=[hbm] * 7,
        out_specs=(vmem, vmem, smem, smem),
        scratch_shapes=[
            pltpu.VMEM((2048, 128), F32),
            pltpu.VMEM(local_gates.shape, F32),
            pltpu.VMEM(top_gates.shape, F32),
            pltpu.SMEM(placement.shape, I32),
            pltpu.SMEM(damping.shape, F32),
            pltpu.SMEM(branches.shape, I32),
            pltpu.SMEM(outcomes.shape, I32),
            pltpu.VMEM((owners * per_block, 128), F32),
            pltpu.VMEM((128 * per_block, 128), F32),
            pltpu.VMEM((8 * per_back, 128), F32),
            pltpu.VMEM((owners * per_back, 128), F32),
            pltpu.VMEM((64, 128), F32),
            pltpu.SemaphoreType.DMA((7,)),
            pltpu.SemaphoreType.DMA((3,)),
            pltpu.SemaphoreType.DMA((3,)),
            pltpu.SemaphoreType.DMA((2,)),
            pltpu.SemaphoreType.REGULAR,
        ],
        compiler_params=pltpu.CompilerParams(
            collective_id=KERNELS.index((level, match)) + 1, has_side_effects=True, vmem_limit_bytes=32 * 1024 * 1024
        ),
        name=f"window{level}",
    )(
        x,
        local_gates,
        top_gates,
        *(
            pltpu.with_memory_space_constraint(small, pltpu.HBM)
            for small in (placement, damping, branches, outcomes)
        ),
    )
    return pl.pallas_call(
        functools.partial(expand_kernel, level),
        out_shape=(
            pltpu.HBM((2048, 128), F32),
            pltpu.HBM((1,), F32),
        ),
        in_specs=[smem, smem, vmem, vmem, hbm],
        out_specs=(hbm, hbm),
        input_output_aliases={4: 0},
        scratch_shapes=[pltpu.VMEM((2048, 128), F32), pltpu.SemaphoreType.DMA((5,))],
        compiler_params=pltpu.CompilerParams(vmem_limit_bytes=32 * 1024 * 1024),
        name=f"expand{level}",
    )(
        chosen,
        probability,
        packed,
        rows,
        pltpu.with_memory_space_constraint(buffer, pltpu.HBM),
    )


def level_kernel(branches_hbm, outcomes_hbm, *rest):
    *choice_refs, out_hbm, branches, outcomes, zeros, in_sem, sems = rest
    loads = [
        pltpu.make_async_copy(branches_hbm, branches, in_sem.at[0]),
        pltpu.make_async_copy(outcomes_hbm, outcomes, in_sem.at[1]),
    ]
    for load in loads:
        load.start()
    zeros[...] = jnp.zeros((256, 128), F32)
    fill_rows(zeros, out_hbm, sems, 0)
    for load in loads:
        load.wait()
    jumps = branches[0]
    for i in range(1, 7):
        jumps = jumps + branches[i]
    choice_refs[4][0] = outcomes[0]
    for limit, choice_ref in enumerate(choice_refs[:4]):
        choice_ref[0] = jnp.where(jumps > limit, 1, 0)


def choose_level(branches, outcomes):
    return pl.pallas_call(
        level_kernel,
        out_shape=(pltpu.SMEM((1,), I32),) * 5 + (pltpu.HBM((2048, 128), F32),),
        in_specs=[pl.BlockSpec(memory_space=pltpu.HBM)] * 2,
        out_specs=(pl.BlockSpec(memory_space=pltpu.SMEM),) * 5
        + (pl.BlockSpec(memory_space=pltpu.HBM),),
        scratch_shapes=[
            pltpu.SMEM((7,), I32),
            pltpu.SMEM((4,), I32),
            pltpu.VMEM((256, 128), F32),
            pltpu.SemaphoreType.DMA((2,)),
            pltpu.SemaphoreType.DMA((4,)),
        ],
        name="level",
    )(branches, outcomes)


def shards(initial_state, *small):
    *more, buffer = choose_level(small[4], small[5])

    def kernel(level, match=None):
        return lambda _, *args: run_level(level, match, *args)

    def choose(choice, otherwise, then):
        return lambda choices, *args: lax.switch(
            choices[choice][0], [otherwise, then], choices, *args
        )

    tree = choose(
        2,
        choose(1, choose(0, kernel(0), kernel(1)), kernel(2)),
        choose(3, kernel(3), choose(4, kernel(4, 0), kernel(4, 1))),
    )
    collapsed, probability = lax.optimization_barrier(
        tree(tuple(more), buffer, initial_state.reshape(2048, 128), *small)
    )
    return collapsed.reshape(initial_state.shape), probability.reshape(())


def solution(mesh):
    return jax.shard_map(
        shards,
        mesh=mesh,
        in_specs=(P(None, "gx", "gy", "gz", None), P(), P(), P(), P(), P(), P()),
        out_specs=(P(None, "gx", "gy", "gz", None), P()),
        check_vma=False,
    )
```

```python
import functools

import jax
import jax.numpy as jnp
from jax import lax
from jax.experimental import pallas as pl
from jax.experimental.pallas import tpu as pltpu
from jax.sharding import PartitionSpec as P

F32 = jnp.float32
BF16 = jnp.bfloat16
I32 = jnp.int32
MESH = pl.DeviceIdType.MESH
TOTAL = 16777216.0


def split(a):
    high = a.astype(BF16)
    return high, (a - high.astype(F32)).astype(BF16)


def mm(a, b, transposed=False):
    dims = (((1,), (1 if transposed else 0,)), ((), ()))
    return lax.dot_general(a, b, dims, preferred_element_type=F32)


def dot_split(a, b, transposed=False):
    return mm(a[0], b[0], transposed) + (mm(a[0], b[1], transposed) + mm(a[1], b[0], transposed))


def dot3(a, b, transposed=False):
    return dot_split(split(a), split(b), transposed)


def permuted_rows(onehot, b):
    high, low = split(b)
    return mm(onehot, high) + mm(onehot, low)


def permuted_columns(a, onehot):
    high, low = split(a)
    return mm(high, onehot) + mm(low, onehot)


def lanes(width=128):
    return lax.broadcasted_iota(I32, (1, width), 1)


def source(legs, k):
    out = jnp.zeros_like(k)
    for i in range(7):
        out = out | (((k >> legs[i]) & 1) << i)
    return out


def unsource(legs, s):
    out = jnp.zeros_like(s)
    for i in range(7):
        out = out | (((s >> i) & 1) << legs[i])
    return out


def hits(target, rows=128):
    return lax.broadcasted_iota(I32, (rows, target.shape[1]), 0) == target


def onehot(target, rows=128):
    return jnp.where(hits(target, rows), 1.0, 0.0).astype(BF16)


def compact_index(branches, j):
    out = jnp.zeros_like(j)
    count = jnp.int32(0)
    for i in range(7):
        stays = 1 - branches[i]
        out = out | ((((j >> i) & 1) * stays) << count)
        count = count + stays
    return out


def kraus_weight(branches, damping, j):
    weight = jnp.ones(j.shape, F32)
    for i in range(7):
        bit = ((j >> i) & 1) == 1
        d = jnp.full(j.shape, damping[i], F32)
        root = jnp.sqrt(jnp.where(branches[i] == 0, 1.0 - d, d))
        off = jnp.where(branches[i] == 0, 1.0, 0.0)
        weight = weight * jnp.where(bit, root, off)
    return weight


def complex_rows(pair):
    half = pair.shape[0] // 2
    r, i = pair[:half], pair[half:]
    return jnp.concatenate(
        [jnp.concatenate([r, -i], axis=1), jnp.concatenate([i, r], axis=1)], axis=0
    )


def complex_columns(pair):
    half = pair.shape[1] // 2
    r, i = pair[:, :half], pair[:, half:]
    return jnp.concatenate(
        [jnp.concatenate([r, i], axis=1), jnp.concatenate([-i, r], axis=1)], axis=0
    )


def side(gate_ref, which):
    return jnp.concatenate([gate_ref[which, 0], gate_ref[which, 1]], axis=1)


def stack_halves(pair):
    half = pair.shape[1] // 2
    return jnp.concatenate([pair[:, :half], pair[:, half:]], axis=0)


def side_halves(pair):
    half = pair.shape[0] // 2
    return jnp.concatenate([pair[:half], pair[half:]], axis=1)


HOPS = (0, 1, 2, 1)


def hops(offset):
    dy, dh, dz, dl = offset
    return HOPS[dy] + HOPS[dz] + (2 if (dh, dl) == (1, 0) else dh | dl)


CHIPS = [
    (dy, dh, dz, dl)
    for dy in range(4)
    for dh in range(2)
    for dz in range(4)
    for dl in range(2)
    if dy or dh or dz or dl
]
FAR = [sorted((o for o in CHIPS if hops(o) in at), key=hops, reverse=True) for at in ((6, 5), (4,))]
NEAR = [[o for o in CHIPS if hops(o) == at] for at in (3, 2, 1)]


def each_core(classes, act):
    for offsets in classes:

        @pl.loop(0, 2)
        def _(other, offsets=offsets):
            for offset in offsets:
                act(offset, other)


OWNERS = [
    (dy, dh, f, dl)
    for dy in range(4)
    for dh in range(2)
    for f in range(2)
    for dl in range(2)
    if dy or dh or f or dl
]
OWNER_CLASSES = [[o for o in OWNERS if hops(o) in at] for at in ((5,), (4,), (3,), (2,), (1,))]


def each_owner(place, act):
    each_core(OWNER_CLASSES, act)
    act((0, 0, 0, 0), 1)

    @pl.when(jnp.logical_not(place.owner))
    def _():
        act((0, 0, 0, 0), 0)


def each_other(act):
    each_core(FAR + NEAR, act)
    act((0, 0, 0, 0), 1)


class Place:
    def __init__(self):
        gx, gy, gz = (lax.axis_index(name) for name in ("gx", "gy", "gz"))
        self.index = (gx * 4 + gy) * 8 + gz
        self.row, self.column = gx * 4 + gy, gz
        self.core, xh = lax.rem(gy, 2), lax.div(gy, 2)
        z, xl = lax.div(gz, 2), lax.rem(gz, 2)
        self.ys = [gx] + [lax.rem(gx + d, 4) for d in (1, 2, 3)]
        zs = [z] + [lax.rem(z + d, 4) for d in (1, 2, 3)]
        self.owner = gz < 4
        self.owner_index = self.row * 4 + gz
        near = lax.div(lax.rem(z + 1, 4), 2)
        owner_zs = [near, 1 - near]
        self.xhs = [xh * 2, 2 - xh * 2]
        xls = [xl, 1 - xl]
        self.gzs = [[zs[dz] * 2 + xls[dl] for dl in range(2)] for dz in range(4)]
        self.owner_gzs = [[owner_zs[f] * 2 + xls[dl] for dl in range(2)] for f in range(2)]

    def device(self, offset, other):
        dy, dh, dz, dl = offset
        core = self.core + other * (1 - 2 * self.core)
        return (self.ys[dy], self.xhs[dh] + core, self.gzs[dz][dl])

    def owner_device(self, offset, other):
        dy, dh, f, dl = offset
        core = self.core + other * (1 - 2 * self.core)
        return (self.ys[dy], self.xhs[dh] + core, self.owner_gzs[f][dl])

    def column_of(self, offset):
        return self.gzs[offset[2]][offset[3]]

    def index_of(self, offset, other):
        gx, gy, gz = self.device(offset, other)
        return (gx * 4 + gy) * 8 + gz


def block(ref, index, rows):
    return ref.at[pl.ds(index * rows, rows)]


def wait_for(ref, rows, sem):
    part = ref.at[pl.ds(0, rows)]
    pltpu.make_async_copy(part, part, sem).wait()


def layout(level):
    shared = level > 3
    return shared, 1 if shared else 2, max(8 >> level, 1), 128 >> level


def main_kernel(
    level,
    match,
    x_hbm,
    local_hbm,
    top_hbm,
    placement_hbm,
    damping_hbm,
    branches_hbm,
    outcomes_hbm,
    f_ref,
    packed_ref,
    chosen_ref,
    p_ref,
    x_ref,
    local_ref,
    top_ref,
    placement,
    damping,
    branches,
    outcomes,
    out_buf,
    in_buf,
    back_out,
    back_in,
    sums_in,
    in_sem,
    send_sem,
    recv_sem,
    own_sem,
    ready_sem,
):
    shared, parts, groups, width = layout(level)
    per_block = 2 if shared else parts * groups
    per_back = per_block + 1
    place = Place()

    barrier = pltpu.get_barrier_semaphore()

    def enter(offset, other):
        pl.semaphore_signal(
            barrier, inc=1, device_id=place.device(offset, other), device_id_type=MESH
        )

    if shared:
        pl.when(place.owner)(lambda: each_other(enter))
    else:
        each_core(FAR, enter)
    loads = [
        pltpu.make_async_copy(src, dst, in_sem.at[n])
        for n, (src, dst) in enumerate(
            (
                (branches_hbm, branches),
                (damping_hbm, damping),
                (placement_hbm, placement),
                (outcomes_hbm, outcomes),
                (local_hbm, local_ref),
                (x_hbm, x_ref),
                (top_hbm, top_ref),
            )
        )
    ]
    for load in loads:
        load.start()
    if not shared:
        each_core(NEAR, enter)
        enter((0, 0, 0, 0), 1)
    for load in loads[:5]:
        load.wait()

    legs = [[placement[t, i] for i in range(7)] for t in range(5)]
    branch = [branches[i] for i in range(7)]
    damp = [damping[i] for i in range(7)]
    lane = lanes()

    after = unsource(legs[3], lane)
    left = jnp.where(
        hits(compact_index(branch, after), width), kraus_weight(branch, damp, after), 0.0
    )
    left = dot3(left, side(local_ref, 2))
    right = permuted_rows(
        onehot(source(legs[3], unsource(legs[0], lane))), side(local_ref, 0)
    )
    right = permuted_columns(stack_halves(right), onehot(source(legs[0], lane)))
    low = stack_halves(dot3(left, complex_columns(side_halves(right))))
    low = split(complex_rows(low))

    middle = unsource(legs[1], lane)
    if shared:
        middle = ((middle >> 2) & 1) * 64 + (middle >> 3) * 4 + (middle & 3)
    mid = permuted_rows(onehot(middle), side(local_ref, 1))
    mid = permuted_columns(stack_halves(mid), onehot(source(legs[1], lane)))
    mid = complex_rows(mid)
    mid = split(mid[:128] if shared else mid)

    loads[5].wait()
    rows = jnp.concatenate(
        [
            jnp.concatenate(
                [x_ref[pl.ds(q, 128, stride=8), :], x_ref[pl.ds(1024 + q, 128, stride=8), :]], axis=1
            )
            for q in range(8)
        ],
        axis=0,
    )
    z = dot_split(low, split(rows), transposed=True)
    for g in range(groups):
        pieces, turned = [], []
        for u in range(8 // groups):
            q = g * (8 // groups) + u
            piece = z[:, q * 128 : q * 128 + 128]
            r, i = piece[:width], piece[width:]
            pieces.append(jnp.concatenate([r, i], axis=1))
            turned.append(jnp.concatenate([i, -r], axis=1))
        if shared:
            pieces = pieces + turned
        y = dot_split(mid, split(jnp.concatenate(pieces, axis=0)), transposed=True)
        if shared:
            for block_of in range(2):
                out_buf[pl.ds(block_of, 64, stride=2), :] = y[block_of * 64 : block_of * 64 + 64]
            continue
        for part in range(parts):
            out_buf[pl.ds(part * groups + g, 128, stride=per_block), :] = y[
                part * 128 : part * 128 + 128
            ]

    if shared:
        pl.when(place.owner)(lambda: pl.semaphore_wait(barrier, 63))
        pl.when(jnp.logical_not(place.owner))(lambda: pl.semaphore_wait(barrier, 64))
    else:
        pl.semaphore_wait(barrier, 127)

    def send(offset, other):
        pltpu.make_async_remote_copy(
            src_ref=block(out_buf, place.index_of(offset, other), per_block),
            dst_ref=block(in_buf, place.index, per_block),
            send_sem=send_sem.at[0],
            recv_sem=recv_sem.at[0],
            device_id=place.device(offset, other),
            device_id_type=MESH,
        ).start()

    slot = place.owner_index if shared else place.index
    own = pltpu.make_async_copy(
        block(out_buf, slot, per_block), block(in_buf, place.index, per_block), own_sem.at[0]
    )

    def send_owner(offset, other):
        gx, gy, gz = device = place.owner_device(offset, other)
        pltpu.make_async_remote_copy(
            src_ref=block(out_buf, (gx * 4 + gy) * 4 + gz, 2),
            dst_ref=block(in_buf, place.index, 2),
            send_sem=send_sem.at[0],
            recv_sem=recv_sem.at[0],
            device_id=device,
            device_id_type=MESH,
        ).start()

    def tell_owner(offset, other):
        pl.semaphore_signal(
            ready_sem, inc=1, device_id=place.owner_device(offset, other), device_id_type=MESH
        )

    if shared:
        each_owner(place, send_owner)
        pl.when(jnp.logical_not(place.owner))(lambda: each_owner(place, tell_owner))
    else:
        each_other(send)
        own.start()

    loads[6].wait()
    zero_row = jnp.zeros_like(lane)
    for n in range(7):
        zero_row = zero_row | (((lane >> n) & 1) * branch[n])
    packed_ref[...] = jnp.where(zero_row == 0, compact_index(branch, lane), -1)

    top = permuted_rows(onehot(unsource(legs[4], lane)), side(top_ref, 1))
    top = permuted_columns(
        stack_halves(top), onehot(source(legs[4], unsource(legs[2], lane)))
    )
    top = dot3(side_halves(top), complex_columns(side(top_ref, 0)))
    top = permuted_columns(stack_halves(top), onehot(source(legs[2], lane)))
    top = split(side_halves(top) if shared else complex_rows(top))
    chosen = outcomes[0] * 8 + outcomes[1] * 4 + outcomes[2] * 2 + outcomes[3]

    first_half = lane < 64

    def send_back(offset, other):
        pltpu.make_async_remote_copy(
            src_ref=block(back_out, place.column_of(offset), per_back),
            dst_ref=block(back_in, slot, per_back),
            send_sem=send_sem.at[1],
            recv_sem=recv_sem.at[1],
            device_id=place.device(offset, other),
            device_id_type=MESH,
        ).start()

    own_back = pltpu.make_async_copy(
        block(back_out, place.column, per_back), block(back_in, slot, per_back), own_sem.at[1]
    )

    total_row = back_out.at[pl.ds(per_block, 1)]
    matches = [lax.div(y, 2) == (0 if match is None else match) for y in place.ys]

    def send_sums(offset, other):
        pltpu.make_async_remote_copy(
            src_ref=total_row,
            dst_ref=block(sums_in, slot, 1),
            send_sem=send_sem.at[2],
            recv_sem=recv_sem.at[2],
            device_id=place.device(offset, other),
            device_id_type=MESH,
        ).start()

    def to_both(dy, act):
        pl.when(matches[dy])(functools.partial(act, send_back))
        pl.when(jnp.logical_not(matches[dy]))(functools.partial(act, send_sums))

    def fold(norm, kept):
        return jnp.where(
            first_half, norm + pltpu.roll(norm, 64, axis=1), kept + pltpu.roll(kept, 64, axis=1)
        )

    def finish(sums, rows):
        sums = jnp.sum(sums, axis=0, keepdims=True)
        norm = jnp.sum(jnp.where(first_half, sums, 0.0), keepdims=True)
        kept = jnp.sum(jnp.where(first_half, 0.0, sums), keepdims=True)
        probability = kept / norm
        scale = jnp.sqrt(TOTAL / norm) / jnp.sqrt(probability)
        for part, first, count, start, value in rows:
            f_ref[part, pl.ds(first, count), pl.ds(start, 128)] = value * scale
        p_ref[0] = jnp.max(probability)
        chosen_ref[0] = jnp.where(chosen == place.row, 1, 0) + jnp.where(p_ref[0] > 0.0, 0, 2)

    if shared:

        @pl.when(place.owner)
        def _():
            own.start()
            own.wait()
            wait_for(in_buf, 127 * 2, recv_sem.at[0])
            columns = []
            for block_of in range(2):
                b = in_buf[pl.ds(block_of, 128, stride=2), :]
                swapped = pltpu.roll(b, 64, axis=1)
                columns.append(
                    jnp.concatenate([b, jnp.where(first_half, -swapped, swapped)], axis=0)
                )
            psi = dot_split(top, split(jnp.concatenate(columns, axis=1)))
            norm = jnp.sum(psi * psi, axis=0, keepdims=True)
            picked = jnp.zeros((8, 256), F32)
            for group in range(16):
                picked = picked + jnp.where(chosen == group, psi[group * 8 : group * 8 + 8], 0.0)
            kept = jnp.sum(picked * picked, axis=0, keepdims=True)
            for block_of in range(2):
                back_out[pl.ds(block_of, 8, stride=3), :] = picked[
                    :, block_of * 128 : block_of * 128 + 128
                ]
            sums = fold(norm[:, :128] + norm[:, 128:], kept[:, :128] + kept[:, 128:])
            back_out[pl.ds(2, 8, stride=3), :] = jnp.broadcast_to(sums, (8, 128))
            pl.semaphore_wait(ready_sem, 64)
            for offsets in FAR + NEAR:
                for dy in (2, 1, 3, 0):
                    group = [o for o in offsets if o[0] == dy]
                    if group:
                        to_both(dy, functools.partial(each_core, [group]))
            to_both(0, lambda act: act((0, 0, 0, 0), 1))

            @pl.when(matches[0])
            def _():
                own_back.start()
                own_back.wait()
                wait_for(back_in, 63 * 3, recv_sem.at[1])

            @pl.when(jnp.logical_not(matches[0]))
            def _():
                own_sums = pltpu.make_async_copy(total_row, block(sums_in, slot, 1), own_sem.at[1])
                own_sums.start()
                own_sums.wait()
                wait_for(sums_in, 63, recv_sem.at[2])

        @pl.when(jnp.logical_not(place.owner))
        def _():
            pl.when(matches[0])(lambda: wait_for(back_in, 64 * 3, recv_sem.at[1]))
            pl.when(jnp.logical_not(matches[0]))(lambda: wait_for(sums_in, 64, recv_sem.at[2]))

        @pl.when(matches[0])
        def _():
            finish(
                back_in[pl.ds(2, 64, stride=3), :],
                [(0, n * 64, 64, 0, back_in[pl.ds(n, 64, stride=3), :]) for n in range(2)],
            )

        @pl.when(jnp.logical_not(matches[0]))
        def _():
            finish(sums_in[...], [])

        @pl.when(place.owner)
        def _():
            wait_for(out_buf, 63 * 2, send_sem.at[0])

            @pl.when(matches[0])
            def _():
                wait_for(x_ref, 63 * 3, send_sem.at[1])
                wait_for(x_ref, 64, send_sem.at[2])

            @pl.when(jnp.logical_not(matches[0]))
            def _():
                wait_for(x_ref, 64 * 3, send_sem.at[1])
                wait_for(x_ref, 63, send_sem.at[2])

        @pl.when(jnp.logical_not(place.owner))
        def _():
            wait_for(out_buf, 64 * 2, send_sem.at[0])

        return

    own.wait()
    wait_for(in_buf, 127 * per_block, recv_sem.at[0])
    norm = jnp.zeros((1, 128), F32)
    kept = jnp.zeros((1, 128), F32)
    for g in range(groups):
        b = [in_buf[pl.ds(part * groups + g, 128, stride=per_block), :] for part in range(parts)]
        psi = dot_split(top, split(jnp.concatenate(b, axis=0)))
        norm = norm + jnp.sum(psi * psi, axis=0, keepdims=True)
        for part in range(parts):
            picked = jnp.zeros((8, 128), F32)
            for group in range(16):
                at = part * 128 + group * 8
                picked = picked + jnp.where(chosen == group, psi[at : at + 8], 0.0)
            kept = kept + jnp.sum(picked * picked, axis=0, keepdims=True)
            back_out[pl.ds(part * groups + g, 8, stride=per_back), :] = picked
    back_out[pl.ds(per_block, 8, stride=per_back), :] = jnp.broadcast_to(fold(norm, kept), (8, 128))
    each_other(send_back)
    own_back.start()
    own_back.wait()
    wait_for(back_in, 127 * per_back, recv_sem.at[1])
    finish(
        back_in[pl.ds(per_block, 128, stride=per_back), :],
        [
            (part, 0, 128, g * 128, back_in[pl.ds(part * groups + g, 128, stride=per_back), :])
            for part in range(parts)
            for g in range(groups)
        ],
    )
    wait_for(out_buf, 127 * per_block, send_sem.at[0])
    wait_for(back_in, 127 * per_back, send_sem.at[1])


def fill_rows(values, out_hbm, sems, first):
    copies = [
        pltpu.make_async_copy(
            values.at[pl.ds(0, 256)], out_hbm.at[pl.ds(first + n * 256, 256)], sems.at[n]
        )
        for n in range(4)
    ]
    for copy in copies:
        copy.start()
    for copy in copies:
        copy.wait()


def expand_kernel(
    level, chosen_ref, p_ref, f_ref, packed_ref, zeros_hbm, out_hbm, p_hbm, buf, sems
):
    shared, parts, groups, width = layout(level)
    each = 8 // groups
    p_copy = pltpu.make_async_copy(p_ref, p_hbm, sems.at[4])
    p_copy.start()
    state = chosen_ref[0]

    @pl.when(lax.rem(state, 2) == 1)
    def _():
        packed = packed_ref[...]
        copies = []
        for part in range(2):
            start = part * 64 if shared else 0
            tables = [
                onehot(jnp.where(packed >= 0, packed + start + u * width, -1)) for u in range(each)
            ]
            for g in range(groups):
                if part < parts:
                    high, low = split(f_ref[part, :, pl.ds(g * 128, 128)])
                if shared and part == 0:
                    lane = lanes()
                    owner = lane & 63
                    order = onehot((owner >> 2) * 8 + (lane >> 6) * 4 + (owner & 3))
                    high, low = mm(order, high).astype(BF16), mm(order, low).astype(BF16)
                for u, table in enumerate(tables):
                    q = g * each + u
                    buf[pl.ds(part * 1024 + q, 128, stride=8), :] = mm(high, table) + mm(low, table)
            here = pl.ds(part * 1024, 1024)
            copies.append(pltpu.make_async_copy(buf.at[here], out_hbm.at[here], sems.at[part]))
            copies[-1].start()
        for copy in copies:
            copy.wait()

    @pl.when(state == 0)
    def _():
        buf[pl.ds(0, 256), :] = jnp.zeros((256, 128), F32)
        fill_rows(buf, out_hbm, sems, 1024)

    @pl.when(state == 2)
    def _():
        buf[...] = jnp.full((2048, 128), jnp.nan, F32)
        copy = pltpu.make_async_copy(buf, out_hbm, sems.at[0])
        copy.start()
        copy.wait()

    p_copy.wait()


KERNELS = ((0, None), (1, None), (2, None), (3, None), (4, 0), (4, 1))


def run_level(level, match, buffer, x, local_gates, top_gates, placement, damping, branches, outcomes):
    shared, parts, groups, _ = layout(level)
    per_block = 2 if shared else parts * groups
    per_back = per_block + 1
    owners = 64 if shared else 128
    vmem = pl.BlockSpec(memory_space=pltpu.VMEM)
    hbm = pl.BlockSpec(memory_space=pltpu.HBM)
    smem = pl.BlockSpec(memory_space=pltpu.SMEM)
    packed, rows, chosen, probability = pl.pallas_call(
        functools.partial(main_kernel, level, match),
        out_shape=(
            pltpu.VMEM((parts, 128, 128 * groups), F32),
            pltpu.VMEM((1, 128), I32),
            pltpu.SMEM((1,), I32),
            pltpu.SMEM((1,), F32),
        ),
        in_specs=[hbm] * 7,
        out_specs=(vmem, vmem, smem, smem),
        scratch_shapes=[
            pltpu.VMEM((2048, 128), F32),
            pltpu.VMEM(local_gates.shape, F32),
            pltpu.VMEM(top_gates.shape, F32),
            pltpu.SMEM(placement.shape, I32),
            pltpu.SMEM(damping.shape, F32),
            pltpu.SMEM(branches.shape, I32),
            pltpu.SMEM(outcomes.shape, I32),
            pltpu.VMEM((owners * per_block, 128), F32),
            pltpu.VMEM((128 * per_block, 128), F32),
            pltpu.VMEM((8 * per_back, 128), F32),
            pltpu.VMEM((owners * per_back, 128), F32),
            pltpu.VMEM((64, 128), F32),
            pltpu.SemaphoreType.DMA((7,)),
            pltpu.SemaphoreType.DMA((3,)),
            pltpu.SemaphoreType.DMA((3,)),
            pltpu.SemaphoreType.DMA((2,)),
            pltpu.SemaphoreType.REGULAR,
        ],
        compiler_params=pltpu.CompilerParams(
            collective_id=KERNELS.index((level, match)) + 1, has_side_effects=True, vmem_limit_bytes=32 * 1024 * 1024
        ),
        name=f"window{level}",
    )(
        x,
        local_gates,
        top_gates,
        *(
            pltpu.with_memory_space_constraint(small, pltpu.HBM)
            for small in (placement, damping, branches, outcomes)
        ),
    )
    return pl.pallas_call(
        functools.partial(expand_kernel, level),
        out_shape=(
            pltpu.HBM((2048, 128), F32),
            pltpu.HBM((1,), F32),
        ),
        in_specs=[smem, smem, vmem, vmem, hbm],
        out_specs=(hbm, hbm),
        input_output_aliases={4: 0},
        scratch_shapes=[pltpu.VMEM((2048, 128), F32), pltpu.SemaphoreType.DMA((5,))],
        compiler_params=pltpu.CompilerParams(vmem_limit_bytes=32 * 1024 * 1024),
        name=f"expand{level}",
    )(
        chosen,
        probability,
        packed,
        rows,
        pltpu.with_memory_space_constraint(buffer, pltpu.HBM),
    )


def level_kernel(branches_hbm, outcomes_hbm, *rest):
    *choice_refs, out_hbm, branches, outcomes, zeros, in_sem, sems = rest
    loads = [
        pltpu.make_async_copy(branches_hbm, branches, in_sem.at[0]),
        pltpu.make_async_copy(outcomes_hbm, outcomes, in_sem.at[1]),
    ]
    for load in loads:
        load.start()
    zeros[...] = jnp.zeros((256, 128), F32)
    fill_rows(zeros, out_hbm, sems, 0)
    for load in loads:
        load.wait()
    jumps = branches[0]
    for i in range(1, 7):
        jumps = jumps + branches[i]
    choice_refs[4][0] = outcomes[0]
    for limit, choice_ref in enumerate(choice_refs[:4]):
        choice_ref[0] = jnp.where(jumps > limit, 1, 0)


def choose_level(branches, outcomes):
    return pl.pallas_call(
        level_kernel,
        out_shape=(pltpu.SMEM((1,), I32),) * 5 + (pltpu.HBM((2048, 128), F32),),
        in_specs=[pl.BlockSpec(memory_space=pltpu.HBM)] * 2,
        out_specs=(pl.BlockSpec(memory_space=pltpu.SMEM),) * 5
        + (pl.BlockSpec(memory_space=pltpu.HBM),),
        scratch_shapes=[
            pltpu.SMEM((7,), I32),
            pltpu.SMEM((4,), I32),
            pltpu.VMEM((256, 128), F32),
            pltpu.SemaphoreType.DMA((2,)),
            pltpu.SemaphoreType.DMA((4,)),
        ],
        name="level",
    )(branches, outcomes)


def shards(initial_state, *small):
    *more, buffer = choose_level(small[4], small[5])

    def kernel(level, match=None):
        return lambda _, *args: run_level(level, match, *args)

    def choose(choice, otherwise, then):
        return lambda choices, *args: lax.switch(
            choices[choice][0], [otherwise, then], choices, *args
        )

    tree = choose(
        2,
        choose(1, choose(0, kernel(0), kernel(1)), kernel(2)),
        choose(3, kernel(3), choose(4, kernel(4, 0), kernel(4, 1))),
    )
    collapsed, probability = lax.optimization_barrier(
        tree(tuple(more), buffer, initial_state.reshape(2048, 128), *small)
    )
    return collapsed.reshape(initial_state.shape), probability.reshape(())


def solution(mesh):
    return jax.shard_map(
        shards,
        mesh=mesh,
        in_specs=(P(None, "gx", "gy", "gz", None), P(), P(), P(), P(), P(), P()),
        out_specs=(P(None, "gx", "gy", "gz", None), P()),
        check_vma=False,
    )
```
